32 devices in a mesh: gx: 8 (over z, x), gy: 4 (over y, core).
Axes of the slice: x: 2, y: 2, z: 4, core: 2. Of those that a mesh axis runs over, the one named last changes fastest.
Arguments:
- states: bfloat16 [2, 64, 8, 64, 512], P(None, None, None, 'gx', 'gy'), may hold values from -6 to 6, as said below
- class_map: int32 [8, 64, 512], P(None, 'gx', 'gy'), may hold values from 0 to 7
- perm_table: float32 [8], replicated, may hold values from 0.05 to 1
- candidates: int32 [8, 4, 64], replicated, may hold values from 0 to 8191, as said below
- merge_order: int32 [31, 128], replicated, may hold values from 0 to 127, each once within a row
Outputs:
- flux: bfloat16 [64, 8, 64, 512], P(None, None, 'gx', 'gy')
- kept_rows: float32 [31, 64, 64], replicated
The draws below stay inside these ranges and needn't reach their ends.
Inputs may be any that keep to these rules, and one draw needn't show every extreme that they name: states[0] is pressure; states[1] is water saturation, between 0.05 and 0.95. `candidates`: each tile's 64 entries are distinct cell numbers (z * 8 + x) * 128 + y of that tile's own cells. `merge_order`: each row is a permutation of 0 to 127.
All inputs are finite; a program needn't handle non-finite values.
Results may differ from the reference program's by a relative error of at most 0.001.
Values may be sent and summed in bfloat16 or wider, within the bound.
A program may use at most 128 MiB of HBM per device.

```python
import math
import jax
import jax.numpy as jnp
from jax import lax

K = 64
NZW = 8
NCLASS = 8
CX = 8
CY = 128
NX = 64
NY = 512
NODES = 31
N_GX = 8
N_GY = 4


def draw_states(key, part):
    key_p = jax.random.fold_in(key, 11)
    key_s = jax.random.fold_in(key, 12)
    shape = (K, NZW, NX, NY)
    pressure = jnp.clip(jax.random.normal(key_p, shape, jnp.float32), -6.0, 6.0)
    saturation = jax.random.uniform(key_s, shape, jnp.float32, 0.1, 0.9)
    return jnp.stack([pressure, saturation]).astype(jnp.bfloat16)


def draw_candidates(key, part):
    cell_count = NZW * CX * CY
    tile_keys = jax.random.split(jax.random.fold_in(key, 21), N_GX * N_GY)
    picked = jax.vmap(lambda one_key: jax.random.permutation(one_key, cell_count)[:K])(tile_keys)
    return picked.reshape(N_GX, N_GY, K).astype(jnp.int32)


def plant(drawn, rng, smallest, largest):
    shape = drawn.shape
    spot = [jax.random.randint(jax.random.fold_in(rng, axis), (), 0, shape[axis]) for axis in range(len(shape))]
    drawn = drawn.at[tuple(spot)].set(smallest)
    longest = shape.index(max(shape))
    spot[longest] = (spot[longest] + 1) % shape[longest]
    return drawn.at[tuple(spot)].set(largest)


def setup_inputs(seed: int = 0) -> dict:
    streams_of = jax.random.split(jax.random.key(seed), 6)
    states = draw_states(jax.random.fold_in(streams_of[5], 71), 0)
    class_map = plant(jax.random.randint(streams_of[1], (NZW, NX, NY), 0, NCLASS), jax.random.fold_in(streams_of[1], 1), 0, NCLASS - 1).astype(jnp.int32)
    perm_table = jnp.clip(jnp.exp(jax.random.uniform(streams_of[2], (NCLASS,), jnp.float32, math.log(0.05), math.log(1.0))), 0.05, 1.0)
    candidates = draw_candidates(jax.random.fold_in(streams_of[5], 71), 0)
    merge_order = jax.vmap(lambda own: jax.random.permutation(own, 2 * K))(jax.random.split(streams_of[4], NODES)).reshape((NODES, 2 * K)).astype(jnp.int32)
    return {"states": states, "class_map": class_map, "perm_table": perm_table, "candidates": candidates, "merge_order": merge_order}


def face_term(p_here, m_here, k_here, p_next, m_next, k_next):
    transmit = 2.0 * k_here * k_next / (k_here + k_next)
    return transmit * (0.5 * (m_here + m_next)) * (p_next - p_here)


def snapshot_flux(pressure, mobility, permeability):
    def rolled(offset_by, along):
        return face_term(pressure, mobility, permeability, jnp.roll(pressure, offset_by, along), jnp.roll(mobility, offset_by, along), jnp.roll(permeability, offset_by, along))

    summed = rolled(-1, 1) + rolled(1, 1)
    summed = summed + rolled(-1, 2)
    summed = summed + rolled(1, 2)
    upper_face = face_term(pressure[:-1], mobility[:-1], permeability[:-1], pressure[1:], mobility[1:], permeability[1:])
    lower_face = face_term(pressure[1:], mobility[1:], permeability[1:], pressure[:-1], mobility[:-1], permeability[:-1])
    zero_plane = jnp.zeros((1,) + pressure.shape[1:], jnp.float32)
    summed = summed + jnp.concatenate([upper_face, zero_plane], axis=0)
    summed = summed + jnp.concatenate([zero_plane, lower_face], axis=0)
    return summed


def tournament(cand_rows, merge_order):
    kept_count = merge_order.shape[1] // 2
    level_rows = cand_rows
    offset = 0
    kept_list = []
    for level_num in range(cand_rows.shape[0].bit_length() - 1):
        groups = level_rows.shape[0] // 2
        paired = level_rows.reshape((groups, 2 * kept_count) + level_rows.shape[2:])
        node_order = merge_order[offset:offset + groups, :kept_count]
        level_rows = jnp.take_along_axis(paired, node_order[:, :, None], axis=1)
        kept_list.append(level_rows)
        offset = offset + groups
    return jnp.concatenate(kept_list, axis=0)


def reference(states, class_map, perm_table, candidates, merge_order):
    permeability = perm_table[class_map]
    tile_area = CX * CY
    tile_x = jnp.arange(N_GX, dtype=jnp.int32)[:, None, None]
    tile_y = jnp.arange(N_GY, dtype=jnp.int32)[None, :, None]
    plane_idx = candidates // tile_area
    within = candidates % tile_area
    glob_x = tile_x * CX + within // CY
    glob_y = tile_y * CY + within % CY
    flat_index = ((plane_idx * NX + glob_x) * NY + glob_y).reshape(-1).astype(jnp.int32)

    def per_snapshot(index):
        snapshot = lax.dynamic_index_in_dim(states, index, 1, keepdims=False)
        pressure = snapshot[0].astype(jnp.float32)
        saturation = snapshot[1].astype(jnp.float32)
        summed = snapshot_flux(pressure, saturation * saturation, permeability)
        return summed.astype(jnp.bfloat16), summed.reshape(-1)[flat_index]

    flux, picked = lax.map(per_snapshot, jnp.arange(K, dtype=jnp.int32))
    cand_rows = jnp.transpose(picked).reshape(N_GX * N_GY, K, K)
    return flux, tournament(cand_rows, merge_order)
```

```python
import functools

import jax
import jax.numpy as jnp
from jax import lax
from jax.experimental import pallas as pl
from jax.experimental.pallas import tpu as pltpu
from jax.sharding import PartitionSpec as P

MESH = pl.DeviceIdType.MESH
F32 = jnp.float32
BF16 = jnp.bfloat16
CHUNKS = 4


def remote(src, dst, send, recv, device):
    return pltpu.make_async_remote_copy(
        src_ref=src, dst_ref=dst, send_sem=send, recv_sem=recv, device_id=device, device_id_type=MESH
    )


def kernel(
    ngx, ngy, k_count, planes, cx, cy,
    states, classes, perm, cands, order, flux_out, kept_out,
    st32, flux32, ksc, tx, ty, tz, xs, xr, kxs, kxr, ys, yr, tcol, ordt, onehot, g1, g2,
    xsend, xrecv, ysend, yrecv, g1send, g1recv, g2send, g2recv, sibsend, sibrecv,
):
    a = lax.axis_index("gx")
    b = lax.axis_index("gy")
    zx = planes * cx
    nodes = ngx * ngy - 1
    per = k_count // CHUNKS
    half = ngy // 4

    barrier = pltpu.get_barrier_semaphore()
    for d in range(1, ngx):
        pl.semaphore_signal(barrier, inc=1, device_id=(lax.rem(a + d, ngx), b), device_id_type=MESH)
    for d in range(1, ngy):
        pl.semaphore_signal(barrier, inc=1, device_id=(a, lax.rem(b + d, ngy)), device_id_type=MESH)

    def to_perm(ids):
        total = jnp.zeros(ids.shape, F32)
        for c in range(perm.shape[0]):
            total = total + jnp.where(ids == c, perm[c], 0.0)
        return total

    k_here = to_perm(classes[...])
    ksc[...] = k_here
    kxs[0] = ksc[pl.ds(0, planes, stride=cx), :]
    kxs[1] = ksc[pl.ds(cx - 1, planes, stride=cx), :]
    x_dev = ((lax.rem(a + ngx - 1, ngx), b), (lax.rem(a + 1, ngx), b))
    y_dev = ((a, lax.rem(b + ngy - 1, ngy)), (a, lax.rem(b + 1, ngy)))

    def x_copy(side, c):
        return remote(xs.at[side, c], xr.at[1 - side, c], xsend.at[side, c], xrecv.at[1 - side, c], x_dev[side])

    def kx_copy(side):
        return remote(
            kxs.at[side], kxr.at[1 - side], xsend.at[side, CHUNKS], xrecv.at[1 - side, CHUNKS], x_dev[side]
        )

    def y_copy(side):
        return remote(ys.at[side], yr.at[1 - side], ysend.at[side], yrecv.at[1 - side], y_dev[side])

    def widen(c):
        def pair(i, carry):
            s0 = c * per + 2 * i
            for q in range(2):
                rows = states[q, pl.ds(pl.multiple_of(s0 * zx, 2 * zx), 2 * zx), :].astype(F32)
                st32[q, pl.ds(pl.multiple_of(s0 * zx, 2 * zx), 2 * zx), :] = rows
                to = pl.ds(pl.multiple_of(q * per * planes + i * 2 * planes, 2 * planes), 2 * planes)
                for side, x in ((0, 0), (1, cx - 1)):
                    edge = st32[q, pl.ds(s0 * zx + x, 2 * planes, stride=cx), :]
                    xs[side, c, to, :] = edge.astype(BF16)
            return carry

        lax.fori_loop(0, per // 2, pair, 0)

    widen(0)
    pl.semaphore_wait(barrier, ngx + ngy - 2)
    for side in range(2):
        kx_copy(side).start()
        x_copy(side, 0).start()
    for c in range(1, CHUNKS):
        widen(c)
        for side in range(2):
            x_copy(side, c).start()

    wide = 8 * zx
    pick_row = lax.broadcasted_iota(jnp.int32, (16, cy), 0)
    pick_lane = lax.broadcasted_iota(jnp.int32, (16, cy), 1)
    first = jnp.where((pick_row == 0) & (pick_lane == 0), 1.0, 0.0)
    last = jnp.where((pick_row == 1) & (pick_lane == cy - 1), 1.0, 0.0)
    pick = (first + last).astype(BF16)
    nt = (((1,), (1,)), ((), ()))
    for j in range(k_count // 8):
        for q in range(2):
            cols = lax.dot_general(pick, states[q, j * wide : (j + 1) * wide, :], nt, preferred_element_type=F32)
            ys[0, q, j : j + 1, :] = cols[0:1, :]
            ys[1, q, j : j + 1, :] = cols[1:2, :]
    ids = classes[...].astype(F32).astype(BF16)
    cols = lax.dot_general(pick, jnp.concatenate([ids] * 8, axis=0), nt, preferred_element_type=F32)
    for side in range(2):
        ys[side, 2] = jnp.broadcast_to(to_perm(cols[side : side + 1, :]), (8, wide))
    for side in range(2):
        y_copy(side).start()

    def transmit(k0, k1):
        return k0 * k1 / (k0 + k1)

    cube = (planes, cx, cy)
    k3 = k_here.reshape(cube)
    sub = lax.broadcasted_iota(jnp.int32, cube, 1)
    lane = lax.broadcasted_iota(jnp.int32, cube, 2)
    tx[...] = jnp.where(sub == cx - 1, 0.0, transmit(k3, pltpu.roll(k3, cx - 1, axis=1)))
    ty[...] = jnp.where(lane == cy - 1, 0.0, transmit(k3, pltpu.roll(k3, cy - 1, axis=2)))
    tz[...] = transmit(k3[:-1], k3[1:])

    def inner(s, carry):
        at = pl.ds(pl.multiple_of(s * zx, zx), zx)
        p = st32[0, at, :].reshape(cube)
        sat = st32[1, at, :].reshape(cube)
        m = sat * sat
        fx = tx[...] * (m + pltpu.roll(m, cx - 1, axis=1)) * (pltpu.roll(p, cx - 1, axis=1) - p)
        fy = ty[...] * (m + pltpu.roll(m, cy - 1, axis=2)) * (pltpu.roll(p, cy - 1, axis=2) - p)
        fz = tz[...] * (m[:-1] + m[1:]) * (p[1:] - p[:-1])
        total = (fx - pltpu.roll(fx, 1, axis=1)) + (fy - pltpu.roll(fy, 1, axis=2))
        zero = jnp.zeros((1, cx, cy), F32)
        total = total + (jnp.concatenate([fz, zero], axis=0) - jnp.concatenate([zero, fz], axis=0))
        flux32[at, :] = total.reshape(zx, cy)
        return carry

    lax.fori_loop(0, k_count, inner, 0)

    ordt[...] = jnp.zeros(ordt.shape, F32)
    ordt[0:nodes, :] = order[...].astype(F32)
    turned = ordt[...].T
    spots = lax.broadcasted_iota(jnp.int32, (k_count, 2 * k_count), 1).astype(F32)
    for n in range(nodes):
        onehot[n] = jnp.where(turned[:k_count, n : n + 1] == spots, 1.0, 0.0).astype(BF16)

    for side in range(2):
        y_copy(side).wait_recv()
    for side in range(2):
        mine, theirs = ys[side, 1], yr[side, 1]
        step = yr[side, 0] - ys[side, 0]
        face = transmit(ys[side, 2], yr[side, 2]) * (mine * mine + theirs * theirs) * step
        tcol[side] = face.T

    for side in range(2):
        kx_copy(side).wait_recv()
    kedge = [transmit(kxs[side], kxr[side]) for side in range(2)]
    kedge = [jnp.concatenate([one, one], axis=0) for one in kedge]
    lane2 = lax.broadcasted_iota(jnp.int32, (2 * zx, cy), 1)
    for c in range(CHUNKS):
        for side in range(2):
            x_copy(side, c).wait_recv()

        for j in range(c * per // 8, (c + 1) * per // 8):
            def outer(i, carry, j=j, c=c):
                s0 = j * 8 + 2 * i
                local = s0 - c * per
                at = pl.ds(pl.multiple_of(s0 * zx, 2 * zx), 2 * zx)
                for side, x in ((0, 0), (1, cx - 1)):
                    rp = pl.ds(pl.multiple_of(local * planes, 2 * planes), 2 * planes)
                    rs = pl.ds(pl.multiple_of((per + local) * planes, 2 * planes), 2 * planes)
                    p0, s_0 = xs[side, c, rp, :].astype(F32), xs[side, c, rs, :].astype(F32)
                    p1, s_1 = xr[side, c, rp, :].astype(F32), xr[side, c, rs, :].astype(F32)
                    face = kedge[side] * (s_0 * s_0 + s_1 * s_1) * (p1 - p0)
                    rows = pl.ds(s0 * zx + x, 2 * planes, stride=cx)
                    flux32[rows, :] = flux32[rows, :] + face
                tat = pl.ds(pl.multiple_of(2 * i * zx, 2 * zx), 2 * zx)
                total = flux32[at, :]
                total = total + jnp.where(lane2 == 0, tcol[0, tat, j : j + 1], 0.0)
                total = total + jnp.where(lane2 == cy - 1, tcol[1, tat, j : j + 1], 0.0)
                flux32[at, :] = total
                flux_out[at, :] = total.astype(BF16)
                return carry

            lax.fori_loop(0, 4, outer, 0)

    lane_k = lax.broadcasted_iota(jnp.int32, (k_count, cy), 1)

    def take(i8, acc):
        for u in range(8):
            i = i8 * 8 + u
            cell = cands[a, b, i]
            row = lax.div(cell, cy)
            col = cell - row * cy
            found = flux32[pl.ds(row, k_count, stride=zx), :]
            value = jnp.sum(jnp.where(lane_k == col, found, 0.0), axis=1, keepdims=True)
            acc = jnp.where(lane_k == i, value, acc)
        return acc

    picked = lax.fori_loop(0, k_count // 8, take, jnp.zeros((k_count, cy), F32)).T[:k_count]
    high = picked.astype(BF16).astype(F32)
    mine = jnp.concatenate([high, picked - high], axis=1).astype(BF16)
    g1[b] = mine

    def g1_copy(d, slot, device):
        return remote(g1.at[slot], g1.at[slot], g1send.at[d], g1recv.at[d], device)

    for d in range(1, ngy):
        g1_copy(d, b, (a, lax.rem(b + d, ngy))).start()
    for d in range(1, ngy):
        g1_copy(d, lax.rem(b + ngy - d, ngy), (a, lax.rem(b + d, ngy))).wait_recv()

    def merge(hot, upper, lower):
        stack = jnp.concatenate([upper, lower], axis=0)
        return jnp.dot(hot, stack, preferred_element_type=F32)

    groups = ngy // 2
    for j in range(groups):
        kept = merge(onehot[a * groups + j], g1[2 * j], g1[2 * j + 1])
        g2[a, j] = kept.astype(BF16)
    core = lax.rem(b, 2)
    twin = (a, b + 1 - 2 * core)
    own = pl.ds(core * half, half)
    other = pl.ds((1 - core) * half, half)

    def g2_copy(d, slot, device):
        return remote(g2.at[slot, own], g2.at[slot, own], g2send.at[d], g2recv.at[d], device)

    def sib_copy(d, slot, part):
        return remote(g2.at[slot, part], g2.at[slot, part], sibsend.at[d], sibrecv.at[d], twin)

    for d in range(1, ngx):
        g2_copy(d, a, (lax.rem(a + d, ngx), b)).start()
    for d in range(1, ngx):
        slot = lax.rem(a + ngx - d, ngx)
        g2_copy(d, slot, (lax.rem(a + d, ngx), b)).wait_recv()
        sib_copy(d, slot, own).start()
    for d in range(1, ngx):
        sib_copy(d, lax.rem(a + ngx - d, ngx), other).wait_recv()

    level = []
    for n in range(ngx * groups):
        rows = g2[n // groups, n % groups]
        level.append(rows)
        wide_rows = rows.astype(F32)
        kept_out[n] = wide_rows[:, :k_count] + wide_rows[:, k_count:]
    n = ngx * groups
    while len(level) > 1:
        following = []
        for j in range(len(level) // 2):
            kept = merge(onehot[n], level[2 * j], level[2 * j + 1])
            kept_out[n] = kept[:, :k_count] + kept[:, k_count:]
            following.append(kept.astype(BF16))
            n += 1
        level = following

    for side in range(2):
        kx_copy(side).wait_send()
        y_copy(side).wait_send()
        for c in range(CHUNKS):
            x_copy(side, c).wait_send()
    for d in range(1, ngy):
        g1_copy(d, b, (a, lax.rem(b + d, ngy))).wait_send()
    for d in range(1, ngx):
        g2_copy(d, a, (lax.rem(a + d, ngx), b)).wait_send()
        sib_copy(d, lax.rem(a + ngx - d, ngx), own).wait_send()


def solution(mesh):
    ngx, ngy = mesh.shape["gx"], mesh.shape["gy"]

    def local(states, class_map, perm_table, candidates, merge_order):
        _, k, planes, cx, cy = states.shape
        zx = planes * cx
        nodes = merge_order.shape[0]
        padded = (nodes + 7) // 8 * 8
        edge = 2 * (k // CHUNKS) * planes
        vmem = pl.BlockSpec(memory_space=pltpu.VMEM)
        smem = pl.BlockSpec(memory_space=pltpu.SMEM)
        dma = pltpu.SemaphoreType.DMA
        flux, kept = pl.pallas_call(
            functools.partial(kernel, ngx, ngy, k, planes, cx, cy),
            out_shape=(
                jax.ShapeDtypeStruct((k * zx, cy), BF16),
                jax.ShapeDtypeStruct((nodes, k, k), F32),
            ),
            in_specs=[vmem, vmem, smem, smem, vmem],
            out_specs=(vmem, vmem),
            scratch_shapes=[
                pltpu.VMEM((2, k * zx, cy), F32),
                pltpu.VMEM((k * zx, cy), F32),
                pltpu.VMEM((zx, cy), F32),
                pltpu.VMEM((planes, cx, cy), F32),
                pltpu.VMEM((planes, cx, cy), F32),
                pltpu.VMEM((planes - 1, cx, cy), F32),
                pltpu.VMEM((2, CHUNKS, edge, cy), BF16),
                pltpu.VMEM((2, CHUNKS, edge, cy), BF16),
                pltpu.VMEM((2, planes, cy), F32),
                pltpu.VMEM((2, planes, cy), F32),
                pltpu.VMEM((2, 3, k // 8, 8 * zx), F32),
                pltpu.VMEM((2, 3, k // 8, 8 * zx), F32),
                pltpu.VMEM((2, 8 * zx, k // 8), F32),
                pltpu.VMEM((padded, 2 * k), F32),
                pltpu.VMEM((nodes, k, 2 * k), BF16),
                pltpu.VMEM((ngy, k, 2 * k), BF16),
                pltpu.VMEM((ngx, ngy // 2, k, 2 * k), BF16),
                dma((2, CHUNKS + 1)),
                dma((2, CHUNKS + 1)),
                dma((2,)),
                dma((2,)),
                dma((ngy,)),
                dma((ngy,)),
                dma((ngx,)),
                dma((ngx,)),
                dma((ngx,)),
                dma((ngx,)),
            ],
            compiler_params=pltpu.CompilerParams(
                collective_id=0, has_side_effects=True, vmem_limit_bytes=48 * 1024 * 1024
            ),
        )(states.reshape(2, k * zx, cy), class_map.reshape(zx, cy), perm_table, candidates, merge_order)
        return flux.reshape(k, planes, cx, cy), kept

    in_specs = (P(None, None, None, "gx", "gy"), P(None, "gx", "gy"), P(), P(), P())
    out_specs = (P(None, None, "gx", "gy"), P())
    return jax.shard_map(local, mesh=mesh, in_specs=in_specs, out_specs=out_specs, check_vma=False)
```

```python
import functools

import jax
import jax.numpy as jnp
from jax import lax
from jax.experimental import pallas as pl
from jax.experimental.pallas import tpu as pltpu
from jax.sharding import PartitionSpec as P

MESH = pl.DeviceIdType.MESH
F32 = jnp.float32
BF16 = jnp.bfloat16
CHUNKS = 4


def remote(src, dst, send, recv, device):
    return pltpu.make_async_remote_copy(
        src_ref=src, dst_ref=dst, send_sem=send, recv_sem=recv, device_id=device, device_id_type=MESH
    )


def kernel(
    ngx, ngy, k_count, planes, cx, cy,
    states_in, classes_in, perm_in, cands_in, order_in, flux_out, kept_out,
    states, classes, perm, cands, order, rowst, insem,
    st32, flux32, ksc, tx, ty, tz, xs, xr, kxs, kxr, ys, yr, tcol, ordt, onehot, g1, g2,
    xsend, xrecv, ysend, yrecv, g1send, g1recv, g2send, g2recv, sibsend, sibrecv,
):
    a = lax.axis_index("gx")
    b = lax.axis_index("gy")
    zx = planes * cx
    nodes = ngx * ngy - 1
    per = k_count // CHUNKS
    half = ngy // 4

    def load(c):
        rows = pl.ds(c * per * zx, per * zx)
        return pltpu.make_async_copy(states_in.at[:, rows], states.at[:, rows], insem.at[c])

    pairs = ((classes_in, classes), (perm_in, perm), (cands_in, cands), (order_in, order))
    small = [pltpu.make_async_copy(src, dst, insem.at[CHUNKS + i]) for i, (src, dst) in enumerate(pairs)]
    load(0).start()
    small[0].start()
    small[1].start()
    for c in range(1, CHUNKS):
        load(c).start()
    small[2].start()
    small[3].start()

    barrier = pltpu.get_barrier_semaphore()
    for d in range(1, ngx):
        pl.semaphore_signal(barrier, inc=1, device_id=(lax.rem(a + d, ngx), b), device_id_type=MESH)
    for d in range(1, ngy):
        pl.semaphore_signal(barrier, inc=1, device_id=(a, lax.rem(b + d, ngy)), device_id_type=MESH)

    def to_perm(ids):
        total = jnp.zeros(ids.shape, F32)
        for c in range(perm.shape[0]):
            total = total + jnp.where(ids == c, perm[c], 0.0)
        return total

    small[0].wait()
    small[1].wait()
    k_here = to_perm(classes[...])
    ksc[...] = k_here
    kxs[0] = ksc[pl.ds(0, planes, stride=cx), :]
    kxs[1] = ksc[pl.ds(cx - 1, planes, stride=cx), :]
    x_dev = ((lax.rem(a + ngx - 1, ngx), b), (lax.rem(a + 1, ngx), b))
    y_dev = ((a, lax.rem(b + ngy - 1, ngy)), (a, lax.rem(b + 1, ngy)))

    def x_copy(side, c):
        return remote(xs.at[side, c], xr.at[1 - side, c], xsend.at[side, c], xrecv.at[1 - side, c], x_dev[side])

    def kx_copy(side):
        return remote(
            kxs.at[side], kxr.at[1 - side], xsend.at[side, CHUNKS], xrecv.at[1 - side, CHUNKS], x_dev[side]
        )

    def y_copy(side):
        return remote(ys.at[side], yr.at[1 - side], ysend.at[side], yrecv.at[1 - side], y_dev[side])

    def widen(c):
        def pair(i, carry):
            s0 = c * per + 2 * i
            for q in range(2):
                rows = states[q, pl.ds(pl.multiple_of(s0 * zx, 2 * zx), 2 * zx), :].astype(F32)
                st32[q, pl.ds(pl.multiple_of(s0 * zx, 2 * zx), 2 * zx), :] = rows
                to = pl.ds(pl.multiple_of(q * per * planes + i * 2 * planes, 2 * planes), 2 * planes)
                for side, x in ((0, 0), (1, cx - 1)):
                    edge = st32[q, pl.ds(s0 * zx + x, 2 * planes, stride=cx), :]
                    xs[side, c, to, :] = edge.astype(BF16)
            return carry

        lax.fori_loop(0, per // 2, pair, 0, unroll=2)

    load(0).wait()
    widen(0)
    pl.semaphore_wait(barrier, ngx + ngy - 2)
    for side in range(2):
        kx_copy(side).start()
        x_copy(side, 0).start()
    for c in range(1, CHUNKS):
        load(c).wait()
        widen(c)
        for side in range(2):
            x_copy(side, c).start()

    wide = 8 * zx
    pick_row = lax.broadcasted_iota(jnp.int32, (16, cy), 0)
    pick_lane = lax.broadcasted_iota(jnp.int32, (16, cy), 1)
    first = jnp.where((pick_row == 0) & (pick_lane == 0), 1.0, 0.0)
    last = jnp.where((pick_row == 1) & (pick_lane == cy - 1), 1.0, 0.0)
    pick = (first + last).astype(BF16)
    nt = (((1,), (1,)), ((), ()))
    for j in range(k_count // 8):
        for q in range(2):
            cols = lax.dot_general(pick, states[q, j * wide : (j + 1) * wide, :], nt, preferred_element_type=F32)
            ys[0, q, j : j + 1, :] = cols[0:1, :]
            ys[1, q, j : j + 1, :] = cols[1:2, :]
    ids = classes[...].astype(F32).astype(BF16)
    cols = lax.dot_general(pick, jnp.concatenate([ids] * 8, axis=0), nt, preferred_element_type=F32)
    for side in range(2):
        ys[side, 2] = jnp.broadcast_to(to_perm(cols[side : side + 1, :]), (8, wide))
    for side in range(2):
        y_copy(side).start()

    def transmit(k0, k1):
        return k0 * k1 / (k0 + k1)

    cube = (planes, cx, cy)
    k3 = k_here.reshape(cube)
    sub = lax.broadcasted_iota(jnp.int32, cube, 1)
    lane = lax.broadcasted_iota(jnp.int32, cube, 2)
    tx[...] = jnp.where(sub == cx - 1, 0.0, transmit(k3, pltpu.roll(k3, cx - 1, axis=1)))
    ty[...] = jnp.where(lane == cy - 1, 0.0, transmit(k3, pltpu.roll(k3, cy - 1, axis=2)))
    tz[...] = transmit(k3[:-1], k3[1:])

    def inner(s, carry):
        at = pl.ds(pl.multiple_of(s * zx, zx), zx)
        p = st32[0, at, :].reshape(cube)
        sat = st32[1, at, :].reshape(cube)
        m = sat * sat
        fx = tx[...] * (m + pltpu.roll(m, cx - 1, axis=1)) * (pltpu.roll(p, cx - 1, axis=1) - p)
        fy = ty[...] * (m + pltpu.roll(m, cy - 1, axis=2)) * (pltpu.roll(p, cy - 1, axis=2) - p)
        fz = tz[...] * (m[:-1] + m[1:]) * (p[1:] - p[:-1])
        total = (fx - pltpu.roll(fx, 1, axis=1)) + (fy - pltpu.roll(fy, 1, axis=2))
        zero = jnp.zeros((1, cx, cy), F32)
        total = total + (jnp.concatenate([fz, zero], axis=0) - jnp.concatenate([zero, fz], axis=0))
        flux32[at, :] = total.reshape(zx, cy)
        return carry

    lax.fori_loop(0, k_count, inner, 0, unroll=2)

    small[3].wait()
    small[2].wait()
    ordt[...] = jnp.zeros(ordt.shape, F32)
    ordt[0:nodes, :] = order[...].astype(F32)
    turned = ordt[...].T
    spots = lax.broadcasted_iota(jnp.int32, (k_count, 2 * k_count), 1).astype(F32)
    for n in range(nodes):
        onehot[n] = jnp.where(turned[:k_count, n : n + 1] == spots, 1.0, 0.0).astype(BF16)

    for side in range(2):
        y_copy(side).wait_recv()
    for side in range(2):
        mine, theirs = ys[side, 1], yr[side, 1]
        step = yr[side, 0] - ys[side, 0]
        face = transmit(ys[side, 2], yr[side, 2]) * (mine * mine + theirs * theirs) * step
        tcol[side] = face.T

    for side in range(2):
        kx_copy(side).wait_recv()
    kedge = [transmit(kxs[side], kxr[side]) for side in range(2)]
    kedge = [jnp.concatenate([one, one], axis=0) for one in kedge]
    lane2 = lax.broadcasted_iota(jnp.int32, (2 * zx, cy), 1)
    lane_k = lax.broadcasted_iota(jnp.int32, (per, cy), 1)
    for c in range(CHUNKS):
        for side in range(2):
            x_copy(side, c).wait_recv()

        for j in range(c * per // 8, (c + 1) * per // 8):
            def outer(i, carry, j=j, c=c):
                s0 = j * 8 + 2 * i
                local = s0 - c * per
                at = pl.ds(s0 * zx, 2 * zx)
                for side, x in ((0, 0), (1, cx - 1)):
                    rp = pl.ds(local * planes, 2 * planes)
                    rs = pl.ds((per + local) * planes, 2 * planes)
                    p0, s_0 = xs[side, c, rp, :].astype(F32), xs[side, c, rs, :].astype(F32)
                    p1, s_1 = xr[side, c, rp, :].astype(F32), xr[side, c, rs, :].astype(F32)
                    face = kedge[side] * (s_0 * s_0 + s_1 * s_1) * (p1 - p0)
                    rows = pl.ds(s0 * zx + x, 2 * planes, stride=cx)
                    flux32[rows, :] = flux32[rows, :] + face
                tat = pl.ds(2 * i * zx, 2 * zx)
                total = flux32[at, :]
                total = total + jnp.where(lane2 == 0, tcol[0, tat, j : j + 1], 0.0)
                total = total + jnp.where(lane2 == cy - 1, tcol[1, tat, j : j + 1], 0.0)
                flux32[at, :] = total
                flux_out[at, :] = total.astype(BF16)
                return carry

            for i in range(4):
                outer(i, 0)

        def take(i16, acc, c=c):
            for u in range(16):
                i = i16 * 16 + u
                cell = cands[a, b, i]
                row = lax.div(cell, cy)
                found = flux32[pl.ds(c * per * zx + row, per, stride=zx), :]
                value = jnp.sum(jnp.where(lane_k == cell - row * cy, found, 0.0), axis=1, keepdims=True)
                acc = jnp.where(lane_k == i, value, acc)
            return acc

        rowst[c * per : (c + 1) * per, :] = lax.fori_loop(0, k_count // 16, take, jnp.zeros((per, cy), F32))

    picked = rowst[...].T[:k_count]
    high = picked.astype(BF16).astype(F32)
    mine = jnp.concatenate([high, picked - high], axis=1).astype(BF16)
    g1[b] = mine

    def g1_copy(d, slot, device):
        return remote(g1.at[slot], g1.at[slot], g1send.at[d], g1recv.at[d], device)

    for d in range(1, ngy):
        g1_copy(d, b, (a, lax.rem(b + d, ngy))).start()
    for d in range(1, ngy):
        g1_copy(d, lax.rem(b + ngy - d, ngy), (a, lax.rem(b + d, ngy))).wait_recv()

    def merge(hot, upper, lower):
        stack = jnp.concatenate([upper, lower], axis=0)
        return jnp.dot(hot, stack, preferred_element_type=F32)

    groups = ngy // 2
    for j in range(groups):
        kept = merge(onehot[a * groups + j], g1[2 * j], g1[2 * j + 1])
        g2[a, j] = kept.astype(BF16)
    core = lax.rem(b, 2)
    twin = (a, b + 1 - 2 * core)
    own = pl.ds(core * half, half)
    other = pl.ds((1 - core) * half, half)

    def g2_copy(d, slot, device):
        return remote(g2.at[slot, own], g2.at[slot, own], g2send.at[d], g2recv.at[d], device)

    def sib_copy(d, slot, part):
        return remote(g2.at[slot, part], g2.at[slot, part], sibsend.at[d], sibrecv.at[d], twin)

    for d in range(1, ngx):
        g2_copy(d, a, (lax.rem(a + d, ngx), b)).start()
    for d in range(1, ngx):
        slot = lax.rem(a + ngx - d, ngx)
        g2_copy(d, slot, (lax.rem(a + d, ngx), b)).wait_recv()
        sib_copy(d, slot, own).start()
    for d in range(1, ngx):
        sib_copy(d, lax.rem(a + ngx - d, ngx), other).wait_recv()

    level = []
    for n in range(ngx * groups):
        rows = g2[n // groups, n % groups]
        level.append(rows)
        wide_rows = rows.astype(F32)
        kept_out[n] = wide_rows[:, :k_count] + wide_rows[:, k_count:]
    n = ngx * groups
    while len(level) > 1:
        following = []
        for j in range(len(level) // 2):
            kept = merge(onehot[n], level[2 * j], level[2 * j + 1])
            kept_out[n] = kept[:, :k_count] + kept[:, k_count:]
            following.append(kept.astype(BF16))
            n += 1
        level = following

    for side in range(2):
        kx_copy(side).wait_send()
        y_copy(side).wait_send()
        for c in range(CHUNKS):
            x_copy(side, c).wait_send()
    for d in range(1, ngy):
        g1_copy(d, b, (a, lax.rem(b + d, ngy))).wait_send()
    for d in range(1, ngx):
        g2_copy(d, a, (lax.rem(a + d, ngx), b)).wait_send()
        sib_copy(d, lax.rem(a + ngx - d, ngx), own).wait_send()


def solution(mesh):
    ngx, ngy = mesh.shape["gx"], mesh.shape["gy"]

    def local(states, class_map, perm_table, candidates, merge_order):
        _, k, planes, cx, cy = states.shape
        zx = planes * cx
        nodes = merge_order.shape[0]
        padded = (nodes + 7) // 8 * 8
        edge = 2 * (k // CHUNKS) * planes
        vmem = pl.BlockSpec(memory_space=pltpu.VMEM)
        hbm = pl.BlockSpec(memory_space=pltpu.HBM)
        dma = pltpu.SemaphoreType.DMA
        flux, kept = pl.pallas_call(
            functools.partial(kernel, ngx, ngy, k, planes, cx, cy),
            out_shape=(
                jax.ShapeDtypeStruct((k * zx, cy), BF16),
                jax.ShapeDtypeStruct((nodes, k, k), F32),
            ),
            in_specs=[hbm] * 5,
            out_specs=(vmem, vmem),
            scratch_shapes=[
                pltpu.VMEM((2, k * zx, cy), BF16),
                pltpu.VMEM((zx, cy), jnp.int32),
                pltpu.SMEM(perm_table.shape, F32),
                pltpu.SMEM(candidates.shape, jnp.int32),
                pltpu.VMEM((nodes, 2 * k), jnp.int32),
                pltpu.VMEM((k, cy), F32),
                dma((CHUNKS + 4,)),
                pltpu.VMEM((2, k * zx, cy), F32),
                pltpu.VMEM((k * zx, cy), F32),
                pltpu.VMEM((zx, cy), F32),
                pltpu.VMEM((planes, cx, cy), F32),
                pltpu.VMEM((planes, cx, cy), F32),
                pltpu.VMEM((planes - 1, cx, cy), F32),
                pltpu.VMEM((2, CHUNKS, edge, cy), BF16),
                pltpu.VMEM((2, CHUNKS, edge, cy), BF16),
                pltpu.VMEM((2, planes, cy), F32),
                pltpu.VMEM((2, planes, cy), F32),
                pltpu.VMEM((2, 3, k // 8, 8 * zx), F32),
                pltpu.VMEM((2, 3, k // 8, 8 * zx), F32),
                pltpu.VMEM((2, 8 * zx, k // 8), F32),
                pltpu.VMEM((padded, 2 * k), F32),
                pltpu.VMEM((nodes, k, 2 * k), BF16),
                pltpu.VMEM((ngy, k, 2 * k), BF16),
                pltpu.VMEM((ngx, ngy // 2, k, 2 * k), BF16),
                dma((2, CHUNKS + 1)),
                dma((2, CHUNKS + 1)),
                dma((2,)),
                dma((2,)),
                dma((ngy,)),
                dma((ngy,)),
                dma((ngx,)),
                dma((ngx,)),
                dma((ngx,)),
                dma((ngx,)),
            ],
            compiler_params=pltpu.CompilerParams(
                collective_id=0, has_side_effects=True, vmem_limit_bytes=48 * 1024 * 1024
            ),
        )(*(
            pltpu.with_memory_space_constraint(x, pltpu.HBM)
            for x in (states.reshape(2, k * zx, cy), class_map.reshape(zx, cy), perm_table, candidates, merge_order)
        ))
        return flux.reshape(k, planes, cx, cy), kept

    in_specs = (P(None, None, None, "gx", "gy"), P(None, "gx", "gy"), P(), P(), P())
    out_specs = (P(None, None, "gx", "gy"), P())
    return jax.shard_map(local, mesh=mesh, in_specs=in_specs, out_specs=out_specs, check_vma=False)
```

```python
import functools

import jax
import jax.numpy as jnp
from jax import lax
from jax.experimental import pallas as pl
from jax.experimental.pallas import tpu as pltpu
from jax.sharding import PartitionSpec as P

MESH = pl.DeviceIdType.MESH
F32 = jnp.float32
BF16 = jnp.bfloat16
CHUNKS = 4


def remote(src, dst, send, recv, device):
    return pltpu.make_async_remote_copy(
        src_ref=src, dst_ref=dst, send_sem=send, recv_sem=recv, device_id=device, device_id_type=MESH
    )


def merge(hot, upper, lower):
    stack = jnp.concatenate([upper, lower], axis=0)
    return jnp.dot(hot, stack, preferred_element_type=F32)


def finish(k_count, flux_in, g2, hots, flux_out, kept_out, kept, sems):
    ngx, groups = g2.shape[:2]
    first = ngx * groups
    put_flux = pltpu.make_async_copy(flux_in, flux_out, sems.at[0])
    put_flux.start()
    level = []
    for n in range(first):
        rows = g2[n // groups, n % groups]
        level.append(rows)
        wide_rows = rows.astype(F32)
        kept[n] = wide_rows[:, :k_count] + wide_rows[:, k_count:]
    put_low = pltpu.make_async_copy(kept.at[pl.ds(0, first)], kept_out.at[pl.ds(0, first)], sems.at[1])
    put_low.start()
    n = first
    while len(level) > 1:
        following = []
        for j in range(len(level) // 2):
            rows = merge(hots[n - first], level[2 * j], level[2 * j + 1])
            kept[n] = rows[:, :k_count] + rows[:, k_count:]
            following.append(rows.astype(BF16))
            n += 1
        level = following
    put_high = pltpu.make_async_copy(
        kept.at[pl.ds(first, n - first)], kept_out.at[pl.ds(first, n - first)], sems.at[2]
    )
    put_high.start()
    put_flux.wait()
    put_low.wait()
    put_high.wait()


def kernel(
    ngx, ngy, k_count, planes, cx, cy,
    states_in, classes_in, perm_in, cands_in, order_in, flux_out, g2, hots,
    states, classes, perm, cands, order, rowst, insem,
    st32, flux32, ksc, tx, ty, tz, xs, xr, kxs, kxr, ys, yr, ky, kyr, yface, ordt, onehot, g1,
    xsend, xrecv, ysend, yrecv, g1send, g1recv, g2send, g2recv, sibsend, sibrecv,
):
    a = lax.axis_index("gx")
    b = lax.axis_index("gy")
    zx = planes * cx
    nodes = ngx * ngy - 1
    per = k_count // CHUNKS
    half = ngy // 4

    def load(c):
        rows = pl.ds(c * per * zx, per * zx)
        return pltpu.make_async_copy(states_in.at[:, rows], states.at[:, rows], insem.at[c])

    pairs = ((classes_in, classes), (perm_in, perm), (cands_in, cands), (order_in, order))
    small = [pltpu.make_async_copy(src, dst, insem.at[CHUNKS + i]) for i, (src, dst) in enumerate(pairs)]
    load(0).start()
    small[0].start()
    small[1].start()
    for c in range(1, CHUNKS):
        load(c).start()
    small[2].start()
    small[3].start()

    barrier = pltpu.get_barrier_semaphore()
    for d in range(1, ngx):
        pl.semaphore_signal(barrier, inc=1, device_id=(lax.rem(a + d, ngx), b), device_id_type=MESH)
    for d in range(1, ngy):
        pl.semaphore_signal(barrier, inc=1, device_id=(a, lax.rem(b + d, ngy)), device_id_type=MESH)

    def to_perm(ids):
        total = jnp.zeros(ids.shape, F32)
        for c in range(perm.shape[0]):
            total = total + jnp.where(ids == c, perm[c], 0.0)
        return total

    small[0].wait()
    small[1].wait()
    k_here = to_perm(classes[...])
    ksc[...] = k_here
    kxs[0] = ksc[pl.ds(0, planes, stride=cx), :]
    kxs[1] = ksc[pl.ds(cx - 1, planes, stride=cx), :]
    x_dev = ((lax.rem(a + ngx - 1, ngx), b), (lax.rem(a + 1, ngx), b))
    y_dev = ((a, lax.rem(b + ngy - 1, ngy)), (a, lax.rem(b + 1, ngy)))

    def x_copy(side, c):
        return remote(xs.at[side, c], xr.at[1 - side, c], xsend.at[side, c], xrecv.at[1 - side, c], x_dev[side])

    def kx_copy(side):
        return remote(
            kxs.at[side], kxr.at[1 - side], xsend.at[side, CHUNKS], xrecv.at[1 - side, CHUNKS], x_dev[side]
        )

    def y_copy(side):
        return remote(ys, yr.at[1 - side], ysend.at[side], yrecv.at[1 - side], y_dev[side])

    def ky_copy(side):
        return remote(ky, kyr.at[1 - side], ysend.at[2 + side], yrecv.at[3 - side], y_dev[side])

    def widen(c):
        def pair(i, carry):
            s0 = c * per + 2 * i
            for q in range(2):
                rows = states[q, pl.ds(pl.multiple_of(s0 * zx, 2 * zx), 2 * zx), :].astype(F32)
                st32[q, pl.ds(pl.multiple_of(s0 * zx, 2 * zx), 2 * zx), :] = rows
                to = pl.ds(pl.multiple_of(q * per * planes + i * 2 * planes, 2 * planes), 2 * planes)
                for side, x in ((0, 0), (1, cx - 1)):
                    edge = st32[q, pl.ds(s0 * zx + x, 2 * planes, stride=cx), :]
                    xs[side, c, to, :] = edge.astype(BF16)
            return carry

        lax.fori_loop(0, per // 2, pair, 0, unroll=2)

    load(0).wait()
    widen(0)
    pl.semaphore_wait(barrier, ngx + ngy - 2)
    for side in range(2):
        kx_copy(side).start()
        x_copy(side, 0).start()
    for c in range(1, CHUNKS):
        load(c).wait()
        widen(c)
        for side in range(2):
            x_copy(side, c).start()

    lane1 = lax.broadcasted_iota(jnp.int32, (cx, cy), 1)

    def pack(plane):
        packed = jnp.zeros((cx, cy), F32)
        for j in range(cy // 2):
            packed = jnp.where((lane1 == 2 * j) | (lane1 == 2 * j + 1), pltpu.roll(plane(j), 2 * j + 1, axis=1), packed)
        return packed

    block = cy // 2 * cx
    blocks = k_count * zx // block

    def pack_block(t, carry):
        def plane(q):
            return lambda j: st32[q, pl.ds(pl.multiple_of(t * block, block) + j * cx, cx), :]

        both = jnp.concatenate([pack(plane(0)), pack(plane(1))], axis=0)
        ys[pl.ds(pl.multiple_of(t * 2 * cx, 2 * cx), 2 * cx), :] = both.astype(BF16)
        return carry

    lax.fori_loop(0, blocks, pack_block, 0)
    ky[...] = pack(lambda j: ksc[j % planes * cx : (j % planes + 1) * cx, :])
    for side in range(2):
        y_copy(side).start()
        ky_copy(side).start()

    def transmit(k0, k1):
        return k0 * k1 / (k0 + k1)

    cube = (planes, cx, cy)
    k3 = k_here.reshape(cube)
    sub = lax.broadcasted_iota(jnp.int32, cube, 1)
    lane = lax.broadcasted_iota(jnp.int32, cube, 2)
    tx[...] = jnp.where(sub == cx - 1, 0.0, transmit(k3, pltpu.roll(k3, cx - 1, axis=1)))
    ty[...] = jnp.where(lane == cy - 1, 0.0, transmit(k3, pltpu.roll(k3, cy - 1, axis=2)))
    tz[...] = transmit(k3[:-1], k3[1:])

    def inner(s, carry):
        at = pl.ds(pl.multiple_of(s * zx, zx), zx)
        p = st32[0, at, :].reshape(cube)
        sat = st32[1, at, :].reshape(cube)
        m = sat * sat
        fx = tx[...] * (m + pltpu.roll(m, cx - 1, axis=1)) * (pltpu.roll(p, cx - 1, axis=1) - p)
        fy = ty[...] * (m + pltpu.roll(m, cy - 1, axis=2)) * (pltpu.roll(p, cy - 1, axis=2) - p)
        fz = tz[...] * (m[:-1] + m[1:]) * (p[1:] - p[:-1])
        total = (fx - pltpu.roll(fx, 1, axis=1)) + (fy - pltpu.roll(fy, 1, axis=2))
        zero = jnp.zeros((1, cx, cy), F32)
        total = total + (jnp.concatenate([fz, zero], axis=0) - jnp.concatenate([zero, fz], axis=0))
        flux32[at, :] = total.reshape(zx, cy)
        return carry

    lax.fori_loop(0, k_count, inner, 0, unroll=2)

    small[3].wait()
    small[2].wait()
    ordt[...] = jnp.zeros(ordt.shape, F32)
    ordt[0:nodes, :] = order[...].astype(F32)
    turned = ordt[...].T
    spots = lax.broadcasted_iota(jnp.int32, (k_count, 2 * k_count), 1).astype(F32)
    for n in range(nodes):
        hot = jnp.where(turned[:k_count, n : n + 1] == spots, 1.0, 0.0).astype(BF16)
        if n < ngx * ngy // 2:
            onehot[n] = hot
        else:
            hots[n - ngx * ngy // 2] = hot

    for side in range(2):
        y_copy(side).wait_recv()
        ky_copy(side).wait_recv()

    def across(low, high):
        return jnp.where(lane1 % 2 == 0, pltpu.roll(high, cy - 1, axis=1), pltpu.roll(low, 1, axis=1))

    kcol = transmit(ky[...], across(kyr[0], kyr[1]))
    for t in range(blocks):
        rows = pl.ds(t * 2 * cx, 2 * cx)
        own, low, high = ys[rows, :].astype(F32), yr[0, rows, :].astype(F32), yr[1, rows, :].astype(F32)
        p1, s_1 = across(low[:cx], high[:cx]), across(low[cx:], high[cx:])
        yface[t] = kcol * (own[cx:] * own[cx:] + s_1 * s_1) * (p1 - own[:cx])

    for side in range(2):
        kx_copy(side).wait_recv()
    kedge = [transmit(kxs[side], kxr[side]) for side in range(2)]
    kedge = [jnp.concatenate([one, one], axis=0) for one in kedge]
    rim = (lane1 == 0) | (lane1 == cy - 1)
    lane_k = lax.broadcasted_iota(jnp.int32, (per, cy), 1)
    for c in range(CHUNKS):
        for side in range(2):
            x_copy(side, c).wait_recv()

        for j in range(c * per // 8, (c + 1) * per // 8):
            def outer(i, carry, j=j, c=c):
                s0 = j * 8 + 2 * i
                local = s0 - c * per
                at = pl.ds(s0 * zx, 2 * zx)
                for side, x in ((0, 0), (1, cx - 1)):
                    rp = pl.ds(local * planes, 2 * planes)
                    rs = pl.ds((per + local) * planes, 2 * planes)
                    p0, s_0 = xs[side, c, rp, :].astype(F32), xs[side, c, rs, :].astype(F32)
                    p1, s_1 = xr[side, c, rp, :].astype(F32), xr[side, c, rs, :].astype(F32)
                    face = kedge[side] * (s_0 * s_0 + s_1 * s_1) * (p1 - p0)
                    rows = pl.ds(s0 * zx + x, 2 * planes, stride=cx)
                    flux32[rows, :] = flux32[rows, :] + face
                fix = []
                for v in range(2 * planes):
                    t, u = divmod(s0 * planes + v, cy // 2)
                    fix.append(jnp.where(rim, pltpu.roll(yface[t], cy - 1 - 2 * u, axis=1), 0.0))
                total = flux32[at, :] + jnp.concatenate(fix, axis=0)
                flux32[at, :] = total
                flux_out[at, :] = total.astype(BF16)
                return carry

            for i in range(4):
                outer(i, 0)

        def take(i16, acc, c=c):
            for u in range(16):
                i = i16 * 16 + u
                cell = cands[a, b, i]
                row = lax.div(cell, cy)
                found = flux32[pl.ds(c * per * zx + row, per, stride=zx), :]
                value = jnp.sum(jnp.where(lane_k == cell - row * cy, found, 0.0), axis=1, keepdims=True)
                acc = jnp.where(lane_k == i, value, acc)
            return acc

        rowst[c * per : (c + 1) * per, :] = lax.fori_loop(0, k_count // 16, take, jnp.zeros((per, cy), F32))

    picked = rowst[...].T[:k_count]
    high = picked.astype(BF16).astype(F32)
    mine = jnp.concatenate([high, picked - high], axis=1).astype(BF16)
    g1[b] = mine

    def g1_copy(d, slot, device):
        return remote(g1.at[slot], g1.at[slot], g1send.at[d], g1recv.at[d], device)

    for d in range(1, ngy):
        g1_copy(d, b, (a, lax.rem(b + d, ngy))).start()
    for d in range(1, ngy):
        g1_copy(d, lax.rem(b + ngy - d, ngy), (a, lax.rem(b + d, ngy))).wait_recv()

    groups = ngy // 2
    for j in range(groups):
        kept = merge(onehot[a * groups + j], g1[2 * j], g1[2 * j + 1])
        g2[a, j] = kept.astype(BF16)
    core = lax.rem(b, 2)
    twin = (a, b + 1 - 2 * core)
    own = pl.ds(core * half, half)
    other = pl.ds((1 - core) * half, half)

    def g2_copy(d, slot, device):
        return remote(g2.at[slot, own], g2.at[slot, own], g2send.at[d], g2recv.at[d], device)

    def sib_copy(d, slot, part):
        return remote(g2.at[slot, part], g2.at[slot, part], sibsend.at[d], sibrecv.at[d], twin)

    for d in range(1, ngx):
        g2_copy(d, a, (lax.rem(a + d, ngx), b)).start()
    for d in range(1, ngx):
        slot = lax.rem(a + ngx - d, ngx)
        g2_copy(d, slot, (lax.rem(a + d, ngx), b)).wait_recv()
        sib_copy(d, slot, own).start()
    for d in range(1, ngx):
        sib_copy(d, lax.rem(a + ngx - d, ngx), other).wait_recv()

    for side in range(2):
        kx_copy(side).wait_send()
        y_copy(side).wait_send()
        ky_copy(side).wait_send()
        for c in range(CHUNKS):
            x_copy(side, c).wait_send()
    for d in range(1, ngy):
        g1_copy(d, b, (a, lax.rem(b + d, ngy))).wait_send()
    for d in range(1, ngx):
        g2_copy(d, a, (lax.rem(a + d, ngx), b)).wait_send()
        sib_copy(d, lax.rem(a + ngx - d, ngx), own).wait_send()


def solution(mesh):
    ngx, ngy = mesh.shape["gx"], mesh.shape["gy"]

    def local(states, class_map, perm_table, candidates, merge_order):
        _, k, planes, cx, cy = states.shape
        zx = planes * cx
        nodes = merge_order.shape[0]
        padded = (nodes + 7) // 8 * 8
        edge = 2 * (k // CHUNKS) * planes
        blocks = k * planes // (cy // 2)
        vmem = pl.BlockSpec(memory_space=pltpu.VMEM)
        hbm = pl.BlockSpec(memory_space=pltpu.HBM)
        dma = pltpu.SemaphoreType.DMA
        tiles = ngx * ngy
        flux, lowest, hots = pl.pallas_call(
            functools.partial(kernel, ngx, ngy, k, planes, cx, cy),
            out_shape=(
                jax.ShapeDtypeStruct((k * zx, cy), BF16),
                jax.ShapeDtypeStruct((ngx, ngy // 2, k, 2 * k), BF16),
                jax.ShapeDtypeStruct((nodes - tiles // 2, k, 2 * k), BF16),
            ),
            in_specs=[hbm] * 5,
            out_specs=(vmem,) * 3,
            scratch_shapes=[
                pltpu.VMEM((2, k * zx, cy), BF16),
                pltpu.VMEM((zx, cy), jnp.int32),
                pltpu.SMEM(perm_table.shape, F32),
                pltpu.SMEM(candidates.shape, jnp.int32),
                pltpu.VMEM((nodes, 2 * k), jnp.int32),
                pltpu.VMEM((k, cy), F32),
                dma((CHUNKS + 4,)),
                pltpu.VMEM((2, k * zx, cy), F32),
                pltpu.VMEM((k * zx, cy), F32),
                pltpu.VMEM((zx, cy), F32),
                pltpu.VMEM((planes, cx, cy), F32),
                pltpu.VMEM((planes, cx, cy), F32),
                pltpu.VMEM((planes - 1, cx, cy), F32),
                pltpu.VMEM((2, CHUNKS, edge, cy), BF16),
                pltpu.VMEM((2, CHUNKS, edge, cy), BF16),
                pltpu.VMEM((2, planes, cy), F32),
                pltpu.VMEM((2, planes, cy), F32),
                pltpu.VMEM((2 * blocks * cx, cy), BF16),
                pltpu.VMEM((2, 2 * blocks * cx, cy), BF16),
                pltpu.VMEM((cx, cy), F32),
                pltpu.VMEM((2, cx, cy), F32),
                pltpu.VMEM((blocks, cx, cy), F32),
                pltpu.VMEM((padded, 2 * k), F32),
                pltpu.VMEM((tiles // 2, k, 2 * k), BF16),
                pltpu.VMEM((ngy, k, 2 * k), BF16),
                dma((2, CHUNKS + 1)),
                dma((2, CHUNKS + 1)),
                dma((4,)),
                dma((4,)),
                dma((ngy,)),
                dma((ngy,)),
                dma((ngx,)),
                dma((ngx,)),
                dma((ngx,)),
                dma((ngx,)),
            ],
            compiler_params=pltpu.CompilerParams(
                collective_id=0, has_side_effects=True, vmem_limit_bytes=32 * 1024 * 1024
            ),
        )(*(
            pltpu.with_memory_space_constraint(x, pltpu.HBM)
            for x in (states.reshape(2, k * zx, cy), class_map.reshape(zx, cy), perm_table, candidates, merge_order)
        ))
        flux, kept = pl.pallas_call(
            functools.partial(finish, k),
            out_shape=(
                jax.ShapeDtypeStruct((k * zx, cy), BF16),
                jax.ShapeDtypeStruct((nodes, k, k), F32),
            ),
            in_specs=[vmem] * 3,
            out_specs=(hbm, hbm),
            scratch_shapes=[pltpu.VMEM((nodes, k, k), F32), dma((3,))],
            compiler_params=pltpu.CompilerParams(vmem_limit_bytes=24 * 1024 * 1024),
        )(flux, lowest, hots)
        return flux.reshape(k, planes, cx, cy), kept

    in_specs = (P(None, None, None, "gx", "gy"), P(None, "gx", "gy"), P(), P(), P())
    out_specs = (P(None, None, "gx", "gy"), P())
    return jax.shard_map(local, mesh=mesh, in_specs=in_specs, out_specs=out_specs, check_vma=False)
```

```python
import functools

import jax
import jax.numpy as jnp
from jax import lax
from jax.experimental import pallas as pl
from jax.experimental.pallas import tpu as pltpu
from jax.sharding import PartitionSpec as P

MESH = pl.DeviceIdType.MESH
F32 = jnp.float32
BF16 = jnp.bfloat16
CHUNKS = 4


def remote(src, dst, send, recv, device):
    return pltpu.make_async_remote_copy(
        src_ref=src, dst_ref=dst, send_sem=send, recv_sem=recv, device_id=device, device_id_type=MESH
    )


def merge(hot, upper, lower):
    stack = jnp.concatenate([upper, lower], axis=0)
    return jnp.dot(hot, stack, preferred_element_type=F32)


def finish(k_count, flux_in, g2, hots, flux_out, kept_out, kept, sems):
    ngx, groups = g2.shape[:2]
    first = ngx * groups
    put_flux = pltpu.make_async_copy(flux_in, flux_out, sems.at[0])
    put_flux.start()
    level = []
    for n in range(first):
        rows = g2[n // groups, n % groups]
        level.append(rows)
        wide_rows = rows.astype(F32)
        kept[n] = wide_rows[:, :k_count] + wide_rows[:, k_count:]
    put_low = pltpu.make_async_copy(kept.at[pl.ds(0, first)], kept_out.at[pl.ds(0, first)], sems.at[1])
    put_low.start()
    n = first
    while len(level) > 1:
        following = []
        for j in range(len(level) // 2):
            rows = merge(hots[n - first], level[2 * j], level[2 * j + 1])
            kept[n] = rows[:, :k_count] + rows[:, k_count:]
            following.append(rows.astype(BF16))
            n += 1
        level = following
    put_high = pltpu.make_async_copy(
        kept.at[pl.ds(first, n - first)], kept_out.at[pl.ds(first, n - first)], sems.at[2]
    )
    put_high.start()
    put_flux.wait()
    put_low.wait()
    put_high.wait()


def kernel(
    ngx, ngy, k_count, planes, cx, cy,
    states_in, classes_in, perm_in, cands_in, order_in, flux_out, g2, hots,
    states, classes, perm, cands, order, rowst, insem,
    st32, flux32, ksc, tx, ty, tz, xs, xr, kxs, kxr, ys, yr, ky, kyr, yface, ke, cs, cr, ordt, onehot, g1,
    csend, crecv, xsend, xrecv, ysend, yrecv, g1send, g1recv, g2send, g2recv, sibsend, sibrecv,
):
    a = lax.axis_index("gx")
    b = lax.axis_index("gy")
    zx = planes * cx
    nodes = ngx * ngy - 1
    per = k_count // CHUNKS
    half = ngy // 4

    def load(c):
        rows = pl.ds(c * per * zx, per * zx)
        return pltpu.make_async_copy(states_in.at[:, rows], states.at[:, rows], insem.at[c])

    pairs = ((classes_in, classes), (perm_in, perm), (cands_in, cands), (order_in, order))
    small = [pltpu.make_async_copy(src, dst, insem.at[CHUNKS + i]) for i, (src, dst) in enumerate(pairs)]
    load(0).start()
    small[0].start()
    small[1].start()
    for c in range(1, CHUNKS):
        load(c).start()
    small[2].start()
    small[3].start()

    barrier = pltpu.get_barrier_semaphore()
    for d in range(1, ngx):
        pl.semaphore_signal(barrier, inc=1, device_id=(lax.rem(a + d, ngx), b), device_id_type=MESH)
    for d in range(1, ngy):
        pl.semaphore_signal(barrier, inc=1, device_id=(a, lax.rem(b + d, ngy)), device_id_type=MESH)

    def to_perm(ids):
        total = jnp.zeros(ids.shape, F32)
        for c in range(perm.shape[0]):
            total = total + jnp.where(ids == c, perm[c], 0.0)
        return total

    small[0].wait()
    small[1].wait()
    k_here = to_perm(classes[...])
    ksc[...] = k_here
    kxs[0] = ksc[pl.ds(0, planes, stride=cx), :]
    kxs[1] = ksc[pl.ds(cx - 1, planes, stride=cx), :]
    x_dev = ((lax.rem(a + ngx - 1, ngx), b), (lax.rem(a + 1, ngx), b))
    y_dev = ((a, lax.rem(b + ngy - 1, ngy)), (a, lax.rem(b + 1, ngy)))

    def x_copy(side, c):
        return remote(xs.at[side, c], xr.at[1 - side, c], xsend.at[side, c], xrecv.at[1 - side, c], x_dev[side])

    def kx_copy(side):
        return remote(
            kxs.at[side], kxr.at[1 - side], xsend.at[side, CHUNKS], xrecv.at[1 - side, CHUNKS], x_dev[side]
        )

    def c_copy(side):
        return remote(cs.at[side], cr.at[1 - side], csend.at[side], crecv.at[1 - side], x_dev[side])

    def y_copy(side):
        return remote(ys, yr.at[1 - side], ysend.at[side], yrecv.at[1 - side], y_dev[side])

    def ky_copy(side):
        return remote(ky, kyr.at[1 - side], ysend.at[2 + side], yrecv.at[3 - side], y_dev[side])

    def widen(c):
        def pair(i, carry):
            s0 = c * per + 2 * i
            for q in range(2):
                rows = states[q, pl.ds(pl.multiple_of(s0 * zx, 2 * zx), 2 * zx), :].astype(F32)
                st32[q, pl.ds(pl.multiple_of(s0 * zx, 2 * zx), 2 * zx), :] = rows
                to = pl.ds(pl.multiple_of(q * per * planes + i * 2 * planes, 2 * planes), 2 * planes)
                for side, x in ((0, 0), (1, cx - 1)):
                    edge = st32[q, pl.ds(s0 * zx + x, 2 * planes, stride=cx), :]
                    xs[side, c, to, :] = edge.astype(BF16)
            return carry

        lax.fori_loop(0, per // 2, pair, 0, unroll=2)

    load(0).wait()
    widen(0)
    pl.semaphore_wait(barrier, ngx + ngy - 2)
    for side in range(2):
        kx_copy(side).start()
        x_copy(side, 0).start()
    for c in range(1, CHUNKS):
        load(c).wait()
        widen(c)
    small[2].wait()
    lane_k = lax.broadcasted_iota(jnp.int32, (k_count, cy), 1)

    def at_cell(ref, row, col):
        found = ref[pl.ds(row, k_count, stride=zx), :]
        return jnp.sum(jnp.where(lane_k == col, found, 0.0), axis=1, keepdims=True)

    blank = jnp.zeros((k_count, cy), F32)
    for side, x in ((0, 0), (1, cx - 1)):
        def lend(i4, acc, side=side, x=x):
            p_acc, s_acc = acc
            for u in range(4):
                i = i4 * 4 + u
                cell = cands[x_dev[side][0], b, i]
                plane = lax.div(cell, cx * cy)
                col = lax.rem(cell, cy)
                p_acc = jnp.where(lane_k == i, at_cell(st32.at[0], plane * cx + x, col), p_acc)
                s_acc = jnp.where(lane_k == i, at_cell(st32.at[1], plane * cx + x, col), s_acc)
            return p_acc, s_acc

        lent_p, lent_s = lax.fori_loop(0, k_count // 4, lend, (blank, blank))
        cs[side, 0:k_count, :] = lent_p.astype(BF16)
        cs[side, k_count : 2 * k_count, :] = lent_s.astype(BF16)
        c_copy(side).start()
    for c in range(1, CHUNKS):
        for side in range(2):
            x_copy(side, c).start()

    lane1 = lax.broadcasted_iota(jnp.int32, (cx, cy), 1)

    def pack(plane):
        packed = jnp.zeros((cx, cy), F32)
        for j in range(cy // 2):
            packed = jnp.where((lane1 == 2 * j) | (lane1 == 2 * j + 1), pltpu.roll(plane(j), 2 * j + 1, axis=1), packed)
        return packed

    block = cy // 2 * cx
    blocks = k_count * zx // block

    def pack_block(t, carry):
        def plane(q):
            return lambda j: st32[q, pl.ds(pl.multiple_of(t * block, block) + j * cx, cx), :]

        both = jnp.concatenate([pack(plane(0)), pack(plane(1))], axis=0)
        ys[pl.ds(pl.multiple_of(t * 2 * cx, 2 * cx), 2 * cx), :] = both.astype(BF16)
        return carry

    lax.fori_loop(0, blocks, pack_block, 0)
    ky[...] = pack(lambda j: ksc[j % planes * cx : (j % planes + 1) * cx, :])
    for side in range(2):
        y_copy(side).start()
        ky_copy(side).start()

    def transmit(k0, k1):
        return k0 * k1 / (k0 + k1)

    cube = (planes, cx, cy)
    k3 = k_here.reshape(cube)
    sub = lax.broadcasted_iota(jnp.int32, cube, 1)
    lane = lax.broadcasted_iota(jnp.int32, cube, 2)
    tx[...] = jnp.where(sub == cx - 1, 0.0, transmit(k3, pltpu.roll(k3, cx - 1, axis=1)))
    ty[...] = jnp.where(lane == cy - 1, 0.0, transmit(k3, pltpu.roll(k3, cy - 1, axis=2)))
    tz[...] = transmit(k3[:-1], k3[1:])

    small[3].wait()
    ordt[...] = jnp.zeros(ordt.shape, F32)
    ordt[0:nodes, :] = order[...].astype(F32)
    turned = ordt[...].T
    spots = lax.broadcasted_iota(jnp.int32, (k_count, 2 * k_count), 1).astype(F32)
    for n in range(nodes):
        hot = jnp.where(turned[:k_count, n : n + 1] == spots, 1.0, 0.0).astype(BF16)
        if n < ngx * ngy // 2:
            onehot[n] = hot
        else:
            hots[n - ngx * ngy // 2] = hot

    for side in range(2):
        y_copy(side).wait_recv()
        ky_copy(side).wait_recv()

    def across(low, high):
        return jnp.where(lane1 % 2 == 0, pltpu.roll(high, cy - 1, axis=1), pltpu.roll(low, 1, axis=1))

    kcol = transmit(ky[...], across(kyr[0], kyr[1]))
    for t in range(blocks):
        rows = pl.ds(t * 2 * cx, 2 * cx)
        own, low, high = ys[rows, :].astype(F32), yr[0, rows, :].astype(F32), yr[1, rows, :].astype(F32)
        p1, s_1 = across(low[:cx], high[:cx]), across(low[cx:], high[cx:])
        yface[t] = kcol * (own[cx:] * own[cx:] + s_1 * s_1) * (p1 - own[:cx])

    rim = (lane1 == 0) | (lane1 == cy - 1)
    in_block = cy // 2 // planes

    def inner(t, carry):
        for u in range(in_block):
            at = pl.ds(pl.multiple_of(t * block, block) + u * zx, zx)
            p = st32[0, at, :].reshape(cube)
            sat = st32[1, at, :].reshape(cube)
            m = sat * sat
            fx = tx[...] * (m + pltpu.roll(m, cx - 1, axis=1)) * (pltpu.roll(p, cx - 1, axis=1) - p)
            fy = ty[...] * (m + pltpu.roll(m, cy - 1, axis=2)) * (pltpu.roll(p, cy - 1, axis=2) - p)
            fz = tz[...] * (m[:-1] + m[1:]) * (p[1:] - p[:-1])
            total = (fx - pltpu.roll(fx, 1, axis=1)) + (fy - pltpu.roll(fy, 1, axis=2))
            zero = jnp.zeros((1, cx, cy), F32)
            total = total + (jnp.concatenate([fz, zero], axis=0) - jnp.concatenate([zero, fz], axis=0))
            face = yface[t]
            fix = []
            for v in range(planes):
                fix.append(jnp.where(rim, pltpu.roll(face, cy - 1 - 2 * (u * planes + v), axis=1), 0.0))
            flux32[at, :] = total.reshape(zx, cy) + jnp.concatenate(fix, axis=0)
        return carry

    lax.fori_loop(0, blocks, inner, 0)

    for side in range(2):
        kx_copy(1 - side).wait_recv()
        ke[side] = transmit(kxs[side], kxr[side])
    lane_1 = lax.broadcasted_iota(jnp.int32, (1, cy), 1)

    def take(i4, acc):
        f_acc, p_acc, s_acc, low_acc, high_acc = acc
        for u in range(4):
            i = i4 * 4 + u
            cell = cands[a, b, i]
            row = lax.div(cell, cy)
            col = cell - row * cy
            plane = lax.div(row, cx)
            x = row - plane * cx
            f_acc = jnp.where(lane_k == i, at_cell(flux32, row, col), f_acc)
            p_acc = jnp.where(lane_k == i, at_cell(st32.at[0], row, col), p_acc)
            s_acc = jnp.where(lane_k == i, at_cell(st32.at[1], row, col), s_acc)
            edge = []
            for side, at_x in ((0, 0), (1, cx - 1)):
                line = ke[side, pl.ds(plane, 1), :]
                value = jnp.sum(jnp.where(lane_1 == col, line, 0.0), axis=1, keepdims=True)
                edge.append(value * (x == at_x).astype(F32))
            low_acc = jnp.where(lane_1 == i, edge[0], low_acc)
            high_acc = jnp.where(lane_1 == i, edge[1], high_acc)
        return f_acc, p_acc, s_acc, low_acc, high_acc

    thin = jnp.zeros((1, cy), F32)
    f_acc, p_acc, s_acc, low_acc, high_acc = lax.fori_loop(
        0, k_count // 4, take, (blank, blank, blank, thin, thin)
    )
    for side, t_acc in ((0, low_acc), (1, high_acc)):
        c_copy(1 - side).wait_recv()
        p1, s_1 = cr[side, 0:k_count, :].astype(F32), cr[side, k_count : 2 * k_count, :].astype(F32)
        f_acc = f_acc + t_acc * (s_acc * s_acc + s_1 * s_1) * (p1 - p_acc)
    picked = f_acc.T[:k_count]
    high = picked.astype(BF16).astype(F32)
    mine = jnp.concatenate([high, picked - high], axis=1).astype(BF16)
    g1[b] = mine

    def g1_copy(d, slot, device):
        return remote(g1.at[slot], g1.at[slot], g1send.at[d], g1recv.at[d], device)

    for d in range(1, ngy):
        g1_copy(d, b, (a, lax.rem(b + d, ngy))).start()

    kedge = [jnp.concatenate([ke[side], ke[side]], axis=0) for side in range(2)]

    def outer(c):
        for side in range(2):
            x_copy(side, c).wait_recv()
        for local in range(0, per, 2):
            s0 = c * per + local
            at = pl.ds(s0 * zx, 2 * zx)
            rp = pl.ds(local * planes, 2 * planes)
            rs = pl.ds((per + local) * planes, 2 * planes)
            for side, x in ((0, 0), (1, cx - 1)):
                p0, s_0 = xs[side, c, rp, :].astype(F32), xs[side, c, rs, :].astype(F32)
                p1, s_1 = xr[side, c, rp, :].astype(F32), xr[side, c, rs, :].astype(F32)
                face = kedge[side] * (s_0 * s_0 + s_1 * s_1) * (p1 - p0)
                rows = pl.ds(s0 * zx + x, 2 * planes, stride=cx)
                flux32[rows, :] = flux32[rows, :] + face
            flux_out[at, :] = flux32[at, :].astype(BF16)

    outer(0)
    for d in range(1, ngy):
        g1_copy(d, lax.rem(b + ngy - d, ngy), (a, lax.rem(b + d, ngy))).wait_recv()

    groups = ngy // 2
    for j in range(groups):
        kept = merge(onehot[a * groups + j], g1[2 * j], g1[2 * j + 1])
        g2[a, j] = kept.astype(BF16)
    core = lax.rem(b, 2)
    twin = (a, b + 1 - 2 * core)
    own = pl.ds(core * half, half)
    other = pl.ds((1 - core) * half, half)

    def g2_copy(d, slot, device):
        return remote(g2.at[slot, own], g2.at[slot, own], g2send.at[d], g2recv.at[d], device)

    def sib_copy(d, slot, part):
        return remote(g2.at[slot, part], g2.at[slot, part], sibsend.at[d], sibrecv.at[d], twin)

    for d in range(1, ngx):
        g2_copy(d, a, (lax.rem(a + d, ngx), b)).start()
    for c in range(1, CHUNKS - 1):
        outer(c)
    for d in range(1, ngx):
        slot = lax.rem(a + ngx - d, ngx)
        g2_copy(d, slot, (lax.rem(a + d, ngx), b)).wait_recv()
        sib_copy(d, slot, own).start()
    outer(CHUNKS - 1)
    for d in range(1, ngx):
        sib_copy(d, lax.rem(a + ngx - d, ngx), other).wait_recv()

    for side in range(2):
        kx_copy(side).wait_send()
        c_copy(side).wait_send()
        y_copy(side).wait_send()
        ky_copy(side).wait_send()
        for c in range(CHUNKS):
            x_copy(side, c).wait_send()
    for d in range(1, ngy):
        g1_copy(d, b, (a, lax.rem(b + d, ngy))).wait_send()
    for d in range(1, ngx):
        g2_copy(d, a, (lax.rem(a + d, ngx), b)).wait_send()
        sib_copy(d, lax.rem(a + ngx - d, ngx), own).wait_send()


def solution(mesh):
    ngx, ngy = mesh.shape["gx"], mesh.shape["gy"]

    def local(states, class_map, perm_table, candidates, merge_order):
        _, k, planes, cx, cy = states.shape
        zx = planes * cx
        nodes = merge_order.shape[0]
        padded = (nodes + 7) // 8 * 8
        edge = 2 * (k // CHUNKS) * planes
        blocks = k * planes // (cy // 2)
        vmem = pl.BlockSpec(memory_space=pltpu.VMEM)
        hbm = pl.BlockSpec(memory_space=pltpu.HBM)
        dma = pltpu.SemaphoreType.DMA
        tiles = ngx * ngy
        flux, lowest, hots = pl.pallas_call(
            functools.partial(kernel, ngx, ngy, k, planes, cx, cy),
            out_shape=(
                jax.ShapeDtypeStruct((k * zx, cy), BF16),
                jax.ShapeDtypeStruct((ngx, ngy // 2, k, 2 * k), BF16),
                jax.ShapeDtypeStruct((nodes - tiles // 2, k, 2 * k), BF16),
            ),
            in_specs=[hbm] * 5,
            out_specs=(vmem,) * 3,
            scratch_shapes=[
                pltpu.VMEM((2, k * zx, cy), BF16),
                pltpu.VMEM((zx, cy), jnp.int32),
                pltpu.SMEM(perm_table.shape, F32),
                pltpu.SMEM(candidates.shape, jnp.int32),
                pltpu.VMEM((nodes, 2 * k), jnp.int32),
                pltpu.VMEM((k, cy), F32),
                dma((CHUNKS + 4,)),
                pltpu.VMEM((2, k * zx, cy), F32),
                pltpu.VMEM((k * zx, cy), F32),
                pltpu.VMEM((zx, cy), F32),
                pltpu.VMEM((planes, cx, cy), F32),
                pltpu.VMEM((planes, cx, cy), F32),
                pltpu.VMEM((planes - 1, cx, cy), F32),
                pltpu.VMEM((2, CHUNKS, edge, cy), BF16),
                pltpu.VMEM((2, CHUNKS, edge, cy), BF16),
                pltpu.VMEM((2, planes, cy), F32),
                pltpu.VMEM((2, planes, cy), F32),
                pltpu.VMEM((2 * blocks * cx, cy), BF16),
                pltpu.VMEM((2, 2 * blocks * cx, cy), BF16),
                pltpu.VMEM((cx, cy), F32),
                pltpu.VMEM((2, cx, cy), F32),
                pltpu.VMEM((blocks, cx, cy), F32),
                pltpu.VMEM((2, planes, cy), F32),
                pltpu.VMEM((2, 2 * k, cy), BF16),
                pltpu.VMEM((2, 2 * k, cy), BF16),
                pltpu.VMEM((padded, 2 * k), F32),
                pltpu.VMEM((tiles // 2, k, 2 * k), BF16),
                pltpu.VMEM((ngy, k, 2 * k), BF16),
                dma((2,)),
                dma((2,)),
                dma((2, CHUNKS + 1)),
                dma((2, CHUNKS + 1)),
                dma((4,)),
                dma((4,)),
                dma((ngy,)),
                dma((ngy,)),
                dma((ngx,)),
                dma((ngx,)),
                dma((ngx,)),
                dma((ngx,)),
            ],
            compiler_params=pltpu.CompilerParams(
                collective_id=0, has_side_effects=True, vmem_limit_bytes=32 * 1024 * 1024
            ),
        )(*(
            pltpu.with_memory_space_constraint(x, pltpu.HBM)
            for x in (states.reshape(2, k * zx, cy), class_map.reshape(zx, cy), perm_table, candidates, merge_order)
        ))
        flux, kept = pl.pallas_call(
            functools.partial(finish, k),
            out_shape=(
                jax.ShapeDtypeStruct((k * zx, cy), BF16),
                jax.ShapeDtypeStruct((nodes, k, k), F32),
            ),
            in_specs=[vmem] * 3,
            out_specs=(hbm, hbm),
            scratch_shapes=[pltpu.VMEM((nodes, k, k), F32), dma((3,))],
            compiler_params=pltpu.CompilerParams(vmem_limit_bytes=24 * 1024 * 1024),
        )(flux, lowest, hots)
        return flux.reshape(k, planes, cx, cy), kept

    in_specs = (P(None, None, None, "gx", "gy"), P(None, "gx", "gy"), P(), P(), P())
    out_specs = (P(None, None, "gx", "gy"), P())
    return jax.shard_map(local, mesh=mesh, in_specs=in_specs, out_specs=out_specs, check_vma=False)
```

```python
import functools

import jax
import jax.numpy as jnp
from jax import lax
from jax.experimental import pallas as pl
from jax.experimental.pallas import tpu as pltpu
from jax.sharding import PartitionSpec as P

MESH = pl.DeviceIdType.MESH
F32 = jnp.float32
BF16 = jnp.bfloat16
CHUNKS = 4


def remote(src, dst, send, recv, device):
    return pltpu.make_async_remote_copy(
        src_ref=src, dst_ref=dst, send_sem=send, recv_sem=recv, device_id=device, device_id_type=MESH
    )


def merge(hot, upper, lower):
    stack = jnp.concatenate([upper, lower], axis=0)
    return jnp.dot(hot, stack, preferred_element_type=F32)


def finish(k_count, flux_in, g2, hots, flux_out, kept_out, kept, sems):
    ngx, groups = g2.shape[:2]
    first = ngx * groups
    put_flux = pltpu.make_async_copy(flux_in, flux_out, sems.at[0])
    put_flux.start()
    level = []
    for n in range(first):
        rows = g2[n // groups, n % groups]
        level.append(rows)
        wide_rows = rows.astype(F32)
        kept[n] = wide_rows[:, :k_count] + wide_rows[:, k_count:]
    put_low = pltpu.make_async_copy(kept.at[pl.ds(0, first)], kept_out.at[pl.ds(0, first)], sems.at[1])
    put_low.start()
    n = first
    while len(level) > 1:
        following = []
        for j in range(len(level) // 2):
            rows = merge(hots[n - first], level[2 * j], level[2 * j + 1])
            kept[n] = rows[:, :k_count] + rows[:, k_count:]
            following.append(rows.astype(BF16))
            n += 1
        level = following
    put_high = pltpu.make_async_copy(
        kept.at[pl.ds(first, n - first)], kept_out.at[pl.ds(first, n - first)], sems.at[2]
    )
    put_high.start()
    put_flux.wait()
    put_low.wait()
    put_high.wait()


def kernel(
    ngx, ngy, k_count, planes, cx, cy,
    states_in, classes_in, perm_in, cands_in, order_in, flux_out, g2, hots,
    states, classes, perm, cands, order, rowst, insem,
    st32, flux32, ksc, tx, ty, tz, xs, xr, kxs, kxr, ys, yr, ky, kyr, yface, ke, cs, cr, ordt, onehot, g1,
    csend, crecv, xsend, xrecv, ysend, yrecv, g1send, g1recv, g2send, g2recv, sibsend, sibrecv,
):
    a = lax.axis_index("gx")
    b = lax.axis_index("gy")
    zx = planes * cx
    nodes = ngx * ngy - 1
    per = k_count // CHUNKS
    half = ngy // 4

    def load(c):
        rows = pl.ds(c * per * zx, per * zx)
        return pltpu.make_async_copy(states_in.at[:, rows], states.at[:, rows], insem.at[c])

    pairs = ((classes_in, classes), (perm_in, perm), (cands_in, cands), (order_in, order))
    small = [pltpu.make_async_copy(src, dst, insem.at[CHUNKS + i]) for i, (src, dst) in enumerate(pairs)]
    load(0).start()
    small[0].start()
    small[1].start()
    for c in range(1, CHUNKS):
        load(c).start()
    small[2].start()
    small[3].start()

    barrier = pltpu.get_barrier_semaphore()
    for d in range(1, ngx):
        pl.semaphore_signal(barrier, inc=1, device_id=(lax.rem(a + d, ngx), b), device_id_type=MESH)
    for d in range(1, ngy):
        pl.semaphore_signal(barrier, inc=1, device_id=(a, lax.rem(b + d, ngy)), device_id_type=MESH)

    def to_perm(ids):
        total = jnp.zeros(ids.shape, F32)
        for c in range(perm.shape[0]):
            total = total + jnp.where(ids == c, perm[c], 0.0)
        return total

    small[0].wait()
    small[1].wait()
    k_here = to_perm(classes[...])
    ksc[...] = k_here
    kxs[0] = ksc[pl.ds(0, planes, stride=cx), :]
    kxs[1] = ksc[pl.ds(cx - 1, planes, stride=cx), :]
    x_dev = ((lax.rem(a + ngx - 1, ngx), b), (lax.rem(a + 1, ngx), b))
    y_dev = ((a, lax.rem(b + ngy - 1, ngy)), (a, lax.rem(b + 1, ngy)))

    def x_copy(side, c):
        return remote(xs.at[side, c], xr.at[1 - side, c], xsend.at[side, c], xrecv.at[1 - side, c], x_dev[side])

    def kx_copy(side):
        return remote(
            kxs.at[side], kxr.at[1 - side], xsend.at[side, CHUNKS], xrecv.at[1 - side, CHUNKS], x_dev[side]
        )

    def c_copy(side):
        return remote(cs.at[side], cr.at[1 - side], csend.at[side], crecv.at[1 - side], x_dev[side])

    def y_copy(side):
        return remote(ys, yr.at[1 - side], ysend.at[side], yrecv.at[1 - side], y_dev[side])

    def ky_copy(side):
        return remote(ky, kyr.at[1 - side], ysend.at[2 + side], yrecv.at[3 - side], y_dev[side])

    def widen(c):
        def pair(i, carry):
            s0 = c * per + 2 * i
            for q in range(2):
                rows = states[q, pl.ds(pl.multiple_of(s0 * zx, 2 * zx), 2 * zx), :].astype(F32)
                st32[q, pl.ds(pl.multiple_of(s0 * zx, 2 * zx), 2 * zx), :] = rows
                to = pl.ds(pl.multiple_of(q * per * planes + i * 2 * planes, 2 * planes), 2 * planes)
                for side, x in ((0, 0), (1, cx - 1)):
                    edge = st32[q, pl.ds(s0 * zx + x, 2 * planes, stride=cx), :]
                    xs[side, c, to, :] = edge.astype(BF16)
            return carry

        lax.fori_loop(0, per // 2, pair, 0, unroll=2)

    load(0).wait()
    widen(0)
    pl.semaphore_wait(barrier, ngx + ngy - 2)
    for side in range(2):
        kx_copy(side).start()
        x_copy(side, 0).start()
    for c in range(1, CHUNKS):
        load(c).wait()
        widen(c)
    small[2].wait()
    lane_k = lax.broadcasted_iota(jnp.int32, (k_count, cy), 1)

    def at_cell(ref, row, turn):
        return pltpu.roll(ref[pl.ds(row, k_count, stride=zx), :], turn, axis=1)

    blank = jnp.zeros((k_count, cy), F32)
    for side, x in ((0, 0), (1, cx - 1)):
        def lend(i4, acc, side=side, x=x):
            p_acc, s_acc = acc
            for u in range(4):
                i = i4 * 4 + u
                cell = cands[x_dev[side][0], b, i]
                plane = lax.div(cell, cx * cy)
                turn = lax.rem(i + cy - lax.rem(cell, cy), cy)
                p_acc = jnp.where(lane_k == i, at_cell(st32.at[0], plane * cx + x, turn), p_acc)
                s_acc = jnp.where(lane_k == i, at_cell(st32.at[1], plane * cx + x, turn), s_acc)
            return p_acc, s_acc

        lent_p, lent_s = lax.fori_loop(0, k_count // 4, lend, (blank, blank))
        cs[side, 0:k_count, :] = lent_p.astype(BF16)
        cs[side, k_count : 2 * k_count, :] = lent_s.astype(BF16)
        c_copy(side).start()
    for c in range(1, CHUNKS):
        for side in range(2):
            x_copy(side, c).start()

    lane1 = lax.broadcasted_iota(jnp.int32, (cx, cy), 1)

    def pack(plane):
        packed = jnp.zeros((cx, cy), F32)
        for j in range(cy // 2):
            packed = jnp.where((lane1 == 2 * j) | (lane1 == 2 * j + 1), pltpu.roll(plane(j), 2 * j + 1, axis=1), packed)
        return packed

    block = cy // 2 * cx
    blocks = k_count * zx // block

    def pack_block(t, carry):
        def plane(q):
            return lambda j: st32[q, pl.ds(pl.multiple_of(t * block, block) + j * cx, cx), :]

        both = jnp.concatenate([pack(plane(0)), pack(plane(1))], axis=0)
        ys[pl.ds(pl.multiple_of(t * 2 * cx, 2 * cx), 2 * cx), :] = both.astype(BF16)
        return carry

    lax.fori_loop(0, blocks, pack_block, 0)
    ky[...] = pack(lambda j: ksc[j % planes * cx : (j % planes + 1) * cx, :])
    for side in range(2):
        y_copy(side).start()
        ky_copy(side).start()

    def transmit(k0, k1):
        return k0 * k1 / (k0 + k1)

    cube = (planes, cx, cy)
    k3 = k_here.reshape(cube)
    sub = lax.broadcasted_iota(jnp.int32, cube, 1)
    lane = lax.broadcasted_iota(jnp.int32, cube, 2)
    tx[...] = jnp.where(sub == cx - 1, 0.0, transmit(k3, pltpu.roll(k3, cx - 1, axis=1)))
    ty[...] = jnp.where(lane == cy - 1, 0.0, transmit(k3, pltpu.roll(k3, cy - 1, axis=2)))
    tz[...] = transmit(k3[:-1], k3[1:])

    small[3].wait()
    ordt[...] = jnp.zeros(ordt.shape, F32)
    ordt[0:nodes, :] = order[...].astype(F32)
    turned = ordt[...].T
    spots = lax.broadcasted_iota(jnp.int32, (k_count, 2 * k_count), 1).astype(F32)
    for n in range(nodes):
        hot = jnp.where(turned[:k_count, n : n + 1] == spots, 1.0, 0.0).astype(BF16)
        if n < ngx * ngy // 2:
            onehot[n] = hot
        else:
            hots[n - ngx * ngy // 2] = hot

    for side in range(2):
        y_copy(side).wait_recv()
        ky_copy(side).wait_recv()

    def across(low, high):
        return jnp.where(lane1 % 2 == 0, pltpu.roll(high, cy - 1, axis=1), pltpu.roll(low, 1, axis=1))

    kcol = transmit(ky[...], across(kyr[0], kyr[1]))
    for t in range(blocks):
        rows = pl.ds(t * 2 * cx, 2 * cx)
        own, low, high = ys[rows, :].astype(F32), yr[0, rows, :].astype(F32), yr[1, rows, :].astype(F32)
        p1, s_1 = across(low[:cx], high[:cx]), across(low[cx:], high[cx:])
        yface[t] = kcol * (own[cx:] * own[cx:] + s_1 * s_1) * (p1 - own[:cx])

    rim = (lane1 == 0) | (lane1 == cy - 1)
    in_block = cy // 2 // planes

    def inner(t, carry):
        for u in range(in_block):
            at = pl.ds(pl.multiple_of(t * block, block) + u * zx, zx)
            p = st32[0, at, :].reshape(cube)
            sat = st32[1, at, :].reshape(cube)
            m = sat * sat
            fx = tx[...] * (m + pltpu.roll(m, cx - 1, axis=1)) * (pltpu.roll(p, cx - 1, axis=1) - p)
            fy = ty[...] * (m + pltpu.roll(m, cy - 1, axis=2)) * (pltpu.roll(p, cy - 1, axis=2) - p)
            fz = tz[...] * (m[:-1] + m[1:]) * (p[1:] - p[:-1])
            total = (fx - pltpu.roll(fx, 1, axis=1)) + (fy - pltpu.roll(fy, 1, axis=2))
            zero = jnp.zeros((1, cx, cy), F32)
            total = total + (jnp.concatenate([fz, zero], axis=0) - jnp.concatenate([zero, fz], axis=0))
            face = yface[t]
            fix = []
            for v in range(planes):
                fix.append(jnp.where(rim, pltpu.roll(face, cy - 1 - 2 * (u * planes + v), axis=1), 0.0))
            flux32[at, :] = total.reshape(zx, cy) + jnp.concatenate(fix, axis=0)
        return carry

    lax.fori_loop(0, blocks, inner, 0)

    for side in range(2):
        kx_copy(1 - side).wait_recv()
        ke[side] = transmit(kxs[side], kxr[side])
    lane_1 = lax.broadcasted_iota(jnp.int32, (1, cy), 1)

    def take(i4, acc):
        f_acc, p_acc, s_acc, low_acc, high_acc = acc
        for u in range(4):
            i = i4 * 4 + u
            cell = cands[a, b, i]
            row = lax.div(cell, cy)
            turn = lax.rem(i + cy - (cell - row * cy), cy)
            plane = lax.div(row, cx)
            x = row - plane * cx
            f_acc = jnp.where(lane_k == i, at_cell(flux32, row, turn), f_acc)
            p_acc = jnp.where(lane_k == i, at_cell(st32.at[0], row, turn), p_acc)
            s_acc = jnp.where(lane_k == i, at_cell(st32.at[1], row, turn), s_acc)
            edge = []
            for side, at_x in ((0, 0), (1, cx - 1)):
                line = pltpu.roll(ke[side, pl.ds(plane, 1), :], turn, axis=1)
                edge.append(line * (x == at_x).astype(F32))
            low_acc = jnp.where(lane_1 == i, edge[0], low_acc)
            high_acc = jnp.where(lane_1 == i, edge[1], high_acc)
        return f_acc, p_acc, s_acc, low_acc, high_acc

    thin = jnp.zeros((1, cy), F32)
    f_acc, p_acc, s_acc, low_acc, high_acc = lax.fori_loop(
        0, k_count // 4, take, (blank, blank, blank, thin, thin)
    )
    for side, t_acc in ((0, low_acc), (1, high_acc)):
        c_copy(1 - side).wait_recv()
        p1, s_1 = cr[side, 0:k_count, :].astype(F32), cr[side, k_count : 2 * k_count, :].astype(F32)
        f_acc = f_acc + t_acc * (s_acc * s_acc + s_1 * s_1) * (p1 - p_acc)
    picked = f_acc.T[:k_count]
    high = picked.astype(BF16).astype(F32)
    mine = jnp.concatenate([high, picked - high], axis=1).astype(BF16)
    g1[b] = mine

    def g1_copy(d, slot, device):
        return remote(g1.at[slot], g1.at[slot], g1send.at[d], g1recv.at[d], device)

    for d in range(1, ngy):
        g1_copy(d, b, (a, lax.rem(b + d, ngy))).start()

    kedge = [jnp.concatenate([ke[side], ke[side]], axis=0) for side in range(2)]

    def outer(c):
        for side in range(2):
            x_copy(side, c).wait_recv()
        for local in range(0, per, 2):
            s0 = c * per + local
            at = pl.ds(s0 * zx, 2 * zx)
            rp = pl.ds(local * planes, 2 * planes)
            rs = pl.ds((per + local) * planes, 2 * planes)
            for side, x in ((0, 0), (1, cx - 1)):
                p0, s_0 = xs[side, c, rp, :].astype(F32), xs[side, c, rs, :].astype(F32)
                p1, s_1 = xr[side, c, rp, :].astype(F32), xr[side, c, rs, :].astype(F32)
                face = kedge[side] * (s_0 * s_0 + s_1 * s_1) * (p1 - p0)
                rows = pl.ds(s0 * zx + x, 2 * planes, stride=cx)
                flux32[rows, :] = flux32[rows, :] + face
            flux_out[at, :] = flux32[at, :].astype(BF16)

    outer(0)
    for d in range(1, ngy):
        g1_copy(d, lax.rem(b + ngy - d, ngy), (a, lax.rem(b + d, ngy))).wait_recv()

    groups = ngy // 2
    for j in range(groups):
        kept = merge(onehot[a * groups + j], g1[2 * j], g1[2 * j + 1])
        g2[a, j] = kept.astype(BF16)
    core = lax.rem(b, 2)
    twin = (a, b + 1 - 2 * core)
    own = pl.ds(core * half, half)
    other = pl.ds((1 - core) * half, half)

    def g2_copy(d, slot, device):
        return remote(g2.at[slot, own], g2.at[slot, own], g2send.at[d], g2recv.at[d], device)

    def sib_copy(d, slot, part):
        return remote(g2.at[slot, part], g2.at[slot, part], sibsend.at[d], sibrecv.at[d], twin)

    for d in range(1, ngx):
        g2_copy(d, a, (lax.rem(a + d, ngx), b)).start()
    for c in range(1, CHUNKS - 1):
        outer(c)
    for d in range(1, ngx):
        slot = lax.rem(a + ngx - d, ngx)
        g2_copy(d, slot, (lax.rem(a + d, ngx), b)).wait_recv()
        sib_copy(d, slot, own).start()
    outer(CHUNKS - 1)
    for d in range(1, ngx):
        sib_copy(d, lax.rem(a + ngx - d, ngx), other).wait_recv()

    for side in range(2):
        kx_copy(side).wait_send()
        c_copy(side).wait_send()
        y_copy(side).wait_send()
        ky_copy(side).wait_send()
        for c in range(CHUNKS):
            x_copy(side, c).wait_send()
    for d in range(1, ngy):
        g1_copy(d, b, (a, lax.rem(b + d, ngy))).wait_send()
    for d in range(1, ngx):
        g2_copy(d, a, (lax.rem(a + d, ngx), b)).wait_send()
        sib_copy(d, lax.rem(a + ngx - d, ngx), own).wait_send()


def solution(mesh):
    ngx, ngy = mesh.shape["gx"], mesh.shape["gy"]

    def local(states, class_map, perm_table, candidates, merge_order):
        _, k, planes, cx, cy = states.shape
        zx = planes * cx
        nodes = merge_order.shape[0]
        padded = (nodes + 7) // 8 * 8
        edge = 2 * (k // CHUNKS) * planes
        blocks = k * planes // (cy // 2)
        vmem = pl.BlockSpec(memory_space=pltpu.VMEM)
        hbm = pl.BlockSpec(memory_space=pltpu.HBM)
        dma = pltpu.SemaphoreType.DMA
        tiles = ngx * ngy
        flux, lowest, hots = pl.pallas_call(
            functools.partial(kernel, ngx, ngy, k, planes, cx, cy),
            out_shape=(
                jax.ShapeDtypeStruct((k * zx, cy), BF16),
                jax.ShapeDtypeStruct((ngx, ngy // 2, k, 2 * k), BF16),
                jax.ShapeDtypeStruct((nodes - tiles // 2, k, 2 * k), BF16),
            ),
            in_specs=[hbm] * 5,
            out_specs=(vmem,) * 3,
            scratch_shapes=[
                pltpu.VMEM((2, k * zx, cy), BF16),
                pltpu.VMEM((zx, cy), jnp.int32),
                pltpu.SMEM(perm_table.shape, F32),
                pltpu.SMEM(candidates.shape, jnp.int32),
                pltpu.VMEM((nodes, 2 * k), jnp.int32),
                pltpu.VMEM((k, cy), F32),
                dma((CHUNKS + 4,)),
                pltpu.VMEM((2, k * zx, cy), F32),
                pltpu.VMEM((k * zx, cy), F32),
                pltpu.VMEM((zx, cy), F32),
                pltpu.VMEM((planes, cx, cy), F32),
                pltpu.VMEM((planes, cx, cy), F32),
                pltpu.VMEM((planes - 1, cx, cy), F32),
                pltpu.VMEM((2, CHUNKS, edge, cy), BF16),
                pltpu.VMEM((2, CHUNKS, edge, cy), BF16),
                pltpu.VMEM((2, planes, cy), F32),
                pltpu.VMEM((2, planes, cy), F32),
                pltpu.VMEM((2 * blocks * cx, cy), BF16),
                pltpu.VMEM((2, 2 * blocks * cx, cy), BF16),
                pltpu.VMEM((cx, cy), F32),
                pltpu.VMEM((2, cx, cy), F32),
                pltpu.VMEM((blocks, cx, cy), F32),
                pltpu.VMEM((2, planes, cy), F32),
                pltpu.VMEM((2, 2 * k, cy), BF16),
                pltpu.VMEM((2, 2 * k, cy), BF16),
                pltpu.VMEM((padded, 2 * k), F32),
                pltpu.VMEM((tiles // 2, k, 2 * k), BF16),
                pltpu.VMEM((ngy, k, 2 * k), BF16),
                dma((2,)),
                dma((2,)),
                dma((2, CHUNKS + 1)),
                dma((2, CHUNKS + 1)),
                dma((4,)),
                dma((4,)),
                dma((ngy,)),
                dma((ngy,)),
                dma((ngx,)),
                dma((ngx,)),
                dma((ngx,)),
                dma((ngx,)),
            ],
            compiler_params=pltpu.CompilerParams(
                collective_id=0, has_side_effects=True, vmem_limit_bytes=32 * 1024 * 1024
            ),
        )(*(
            pltpu.with_memory_space_constraint(x, pltpu.HBM)
            for x in (states.reshape(2, k * zx, cy), class_map.reshape(zx, cy), perm_table, candidates, merge_order)
        ))
        flux, kept = pl.pallas_call(
            functools.partial(finish, k),
            out_shape=(
                jax.ShapeDtypeStruct((k * zx, cy), BF16),
                jax.ShapeDtypeStruct((nodes, k, k), F32),
            ),
            in_specs=[vmem] * 3,
            out_specs=(hbm, hbm),
            scratch_shapes=[pltpu.VMEM((nodes, k, k), F32), dma((3,))],
            compiler_params=pltpu.CompilerParams(vmem_limit_bytes=24 * 1024 * 1024),
        )(flux, lowest, hots)
        return flux.reshape(k, planes, cx, cy), kept

    in_specs = (P(None, None, None, "gx", "gy"), P(None, "gx", "gy"), P(), P(), P())
    out_specs = (P(None, None, "gx", "gy"), P())
    return jax.shard_map(local, mesh=mesh, in_specs=in_specs, out_specs=out_specs, check_vma=False)
```

```python
import functools

import jax
import jax.numpy as jnp
from jax import lax
from jax.experimental import pallas as pl
from jax.experimental.pallas import tpu as pltpu
from jax.sharding import PartitionSpec as P

MESH = pl.DeviceIdType.MESH
F32 = jnp.float32
BF16 = jnp.bfloat16
CHUNKS = 8


def remote(src, dst, send, recv, device):
    return pltpu.make_async_remote_copy(
        src_ref=src, dst_ref=dst, send_sem=send, recv_sem=recv, device_id=device, device_id_type=MESH
    )


def merge(hot, upper, lower):
    stack = jnp.concatenate([upper, lower], axis=0)
    return jnp.dot(hot, stack, preferred_element_type=F32)


def finish(k_count, flux_in, g2, hots, flux_out, kept_out, kept, sems):
    ngx, groups = g2.shape[:2]
    first = ngx * groups
    put_flux = pltpu.make_async_copy(flux_in, flux_out, sems.at[0])
    put_flux.start()
    level = []
    for n in range(first):
        rows = g2[n // groups, n % groups]
        level.append(rows)
        wide_rows = rows.astype(F32)
        kept[n] = wide_rows[:, :k_count] + wide_rows[:, k_count:]
    put_low = pltpu.make_async_copy(kept.at[pl.ds(0, first)], kept_out.at[pl.ds(0, first)], sems.at[1])
    put_low.start()
    n = first
    while len(level) > 1:
        following = []
        for j in range(len(level) // 2):
            rows = merge(hots[n - first], level[2 * j], level[2 * j + 1])
            kept[n] = rows[:, :k_count] + rows[:, k_count:]
            following.append(rows.astype(BF16))
            n += 1
        level = following
    put_high = pltpu.make_async_copy(
        kept.at[pl.ds(first, n - first)], kept_out.at[pl.ds(first, n - first)], sems.at[2]
    )
    put_high.start()
    put_flux.wait()
    put_low.wait()
    put_high.wait()


def kernel(
    ngx, ngy, k_count, planes, cx, cy,
    states_in, classes_in, perm_in, cands_in, order_in, flux_out, g2, hots,
    states, classes, perm, cands, order, rowst, insem,
    st32, flux32, ksc, tx, ty, tz, xs, xr, kxs, kxr, ys, yr, ky, kyr, yface, ordt, onehot, g1,
    xsend, xrecv, ysend, yrecv, g1send, g1recv, g2send, g2recv, sibsend, sibrecv,
):
    a = lax.axis_index("gx")
    b = lax.axis_index("gy")
    zx = planes * cx
    nodes = ngx * ngy - 1
    per = k_count // CHUNKS
    half = ngy // 4

    def load(c):
        rows = pl.ds(c * per * zx, per * zx)
        return pltpu.make_async_copy(states_in.at[:, rows], states.at[:, rows], insem.at[c])

    pairs = ((classes_in, classes), (perm_in, perm), (cands_in, cands), (order_in, order))
    small = [pltpu.make_async_copy(src, dst, insem.at[CHUNKS + i]) for i, (src, dst) in enumerate(pairs)]
    load(0).start()
    small[0].start()
    small[1].start()
    for c in range(1, CHUNKS):
        load(c).start()
    small[2].start()
    small[3].start()

    barrier = pltpu.get_barrier_semaphore()
    for d in range(1, ngx):
        pl.semaphore_signal(barrier, inc=1, device_id=(lax.rem(a + d, ngx), b), device_id_type=MESH)
    for d in range(1, ngy):
        pl.semaphore_signal(barrier, inc=1, device_id=(a, lax.rem(b + d, ngy)), device_id_type=MESH)

    def to_perm(ids):
        total = jnp.zeros(ids.shape, F32)
        for c in range(perm.shape[0]):
            total = total + jnp.where(ids == c, perm[c], 0.0)
        return total

    small[0].wait()
    small[1].wait()
    k_here = to_perm(classes[...])
    ksc[...] = k_here
    kxs[0] = ksc[pl.ds(0, planes, stride=cx), :]
    kxs[1] = ksc[pl.ds(cx - 1, planes, stride=cx), :]
    x_dev = ((lax.rem(a + ngx - 1, ngx), b), (lax.rem(a + 1, ngx), b))
    y_dev = ((a, lax.rem(b + ngy - 1, ngy)), (a, lax.rem(b + 1, ngy)))

    def x_copy(side, c):
        return remote(xs.at[side, c], xr.at[1 - side, c], xsend.at[side, c], xrecv.at[1 - side, c], x_dev[side])

    def kx_copy(side):
        return remote(
            kxs.at[side], kxr.at[1 - side], xsend.at[side, CHUNKS], xrecv.at[1 - side, CHUNKS], x_dev[side]
        )

    def y_copy(side):
        return remote(ys, yr.at[1 - side], ysend.at[side], yrecv.at[1 - side], y_dev[side])

    def ky_copy(side):
        return remote(ky, kyr.at[1 - side], ysend.at[2 + side], yrecv.at[3 - side], y_dev[side])

    def widen(c):
        def pair(i, carry):
            s0 = c * per + 2 * i
            for q in range(2):
                rows = states[q, pl.ds(pl.multiple_of(s0 * zx, 2 * zx), 2 * zx), :].astype(F32)
                st32[q, pl.ds(pl.multiple_of(s0 * zx, 2 * zx), 2 * zx), :] = rows
                to = pl.ds(pl.multiple_of(q * per * planes + i * 2 * planes, 2 * planes), 2 * planes)
                for side, x in ((0, 0), (1, cx - 1)):
                    edge = st32[q, pl.ds(s0 * zx + x, 2 * planes, stride=cx), :]
                    xs[side, c, to, :] = edge.astype(BF16)
            return carry

        lax.fori_loop(0, per // 2, pair, 0, unroll=2)

    load(0).wait()
    widen(0)
    pl.semaphore_wait(barrier, ngx + ngy - 2)
    for side in range(2):
        kx_copy(side).start()
        x_copy(side, 0).start()
    for c in range(1, CHUNKS):
        load(c).wait()
        widen(c)
        for side in range(2):
            x_copy(side, c).start()

    lane1 = lax.broadcasted_iota(jnp.int32, (cx, cy), 1)

    def pack(plane):
        packed = jnp.zeros((cx, cy), F32)
        for j in range(cy // 2):
            packed = jnp.where((lane1 == 2 * j) | (lane1 == 2 * j + 1), pltpu.roll(plane(j), 2 * j + 1, axis=1), packed)
        return packed

    block = cy // 2 * cx
    blocks = k_count * zx // block

    def pack_block(t, carry):
        def plane(q):
            return lambda j: st32[q, pl.ds(pl.multiple_of(t * block, block) + j * cx, cx), :]

        both = jnp.concatenate([pack(plane(0)), pack(plane(1))], axis=0)
        ys[pl.ds(pl.multiple_of(t * 2 * cx, 2 * cx), 2 * cx), :] = both.astype(BF16)
        return carry

    lax.fori_loop(0, blocks, pack_block, 0)
    ky[...] = pack(lambda j: ksc[j % planes * cx : (j % planes + 1) * cx, :])
    for side in range(2):
        y_copy(side).start()
        ky_copy(side).start()

    def transmit(k0, k1):
        return k0 * k1 / (k0 + k1)

    cube = (planes, cx, cy)
    k3 = k_here.reshape(cube)
    sub = lax.broadcasted_iota(jnp.int32, cube, 1)
    lane = lax.broadcasted_iota(jnp.int32, cube, 2)
    tx[...] = jnp.where(sub == cx - 1, 0.0, transmit(k3, pltpu.roll(k3, cx - 1, axis=1)))
    ty[...] = jnp.where(lane == cy - 1, 0.0, transmit(k3, pltpu.roll(k3, cy - 1, axis=2)))
    tz[...] = transmit(k3[:-1], k3[1:])

    def inner(s, carry):
        at = pl.ds(pl.multiple_of(s * zx, zx), zx)
        p = st32[0, at, :].reshape(cube)
        sat = st32[1, at, :].reshape(cube)
        m = sat * sat
        fx = tx[...] * (m + pltpu.roll(m, cx - 1, axis=1)) * (pltpu.roll(p, cx - 1, axis=1) - p)
        fy = ty[...] * (m + pltpu.roll(m, cy - 1, axis=2)) * (pltpu.roll(p, cy - 1, axis=2) - p)
        fz = tz[...] * (m[:-1] + m[1:]) * (p[1:] - p[:-1])
        total = (fx - pltpu.roll(fx, 1, axis=1)) + (fy - pltpu.roll(fy, 1, axis=2))
        zero = jnp.zeros((1, cx, cy), F32)
        total = total + (jnp.concatenate([fz, zero], axis=0) - jnp.concatenate([zero, fz], axis=0))
        flux32[at, :] = total.reshape(zx, cy)
        return carry

    lax.fori_loop(0, k_count, inner, 0, unroll=2)

    small[3].wait()
    small[2].wait()
    ordt[...] = jnp.zeros(ordt.shape, F32)
    ordt[0:nodes, :] = order[...].astype(F32)
    turned = ordt[...].T
    spots = lax.broadcasted_iota(jnp.int32, (k_count, 2 * k_count), 1).astype(F32)
    for n in range(nodes):
        hot = jnp.where(turned[:k_count, n : n + 1] == spots, 1.0, 0.0).astype(BF16)
        if n < ngx * ngy // 2:
            onehot[n] = hot
        else:
            hots[n - ngx * ngy // 2] = hot

    for side in range(2):
        y_copy(side).wait_recv()
        ky_copy(side).wait_recv()

    def across(low, high):
        return jnp.where(lane1 % 2 == 0, pltpu.roll(high, cy - 1, axis=1), pltpu.roll(low, 1, axis=1))

    kcol = transmit(ky[...], across(kyr[0], kyr[1]))
    for t in range(blocks):
        rows = pl.ds(t * 2 * cx, 2 * cx)
        own, low, high = ys[rows, :].astype(F32), yr[0, rows, :].astype(F32), yr[1, rows, :].astype(F32)
        p1, s_1 = across(low[:cx], high[:cx]), across(low[cx:], high[cx:])
        yface[t] = kcol * (own[cx:] * own[cx:] + s_1 * s_1) * (p1 - own[:cx])

    for side in range(2):
        kx_copy(side).wait_recv()
    kedge = [transmit(kxs[side], kxr[side]) for side in range(2)]
    kedge = [jnp.concatenate([one, one], axis=0) for one in kedge]
    rim = (lane1 == 0) | (lane1 == cy - 1)
    lane_k = lax.broadcasted_iota(jnp.int32, (per, cy), 1)
    for c in range(CHUNKS):
        for side in range(2):
            x_copy(side, c).wait_recv()

        for j in range(c * per // 8, (c + 1) * per // 8):
            def outer(i, carry, j=j, c=c):
                s0 = j * 8 + 2 * i
                local = s0 - c * per
                at = pl.ds(s0 * zx, 2 * zx)
                for side, x in ((0, 0), (1, cx - 1)):
                    rp = pl.ds(local * planes, 2 * planes)
                    rs = pl.ds((per + local) * planes, 2 * planes)
                    p0, s_0 = xs[side, c, rp, :].astype(F32), xs[side, c, rs, :].astype(F32)
                    p1, s_1 = xr[side, c, rp, :].astype(F32), xr[side, c, rs, :].astype(F32)
                    face = kedge[side] * (s_0 * s_0 + s_1 * s_1) * (p1 - p0)
                    rows = pl.ds(s0 * zx + x, 2 * planes, stride=cx)
                    flux32[rows, :] = flux32[rows, :] + face
                fix = []
                for v in range(2 * planes):
                    t, u = divmod(s0 * planes + v, cy // 2)
                    fix.append(jnp.where(rim, pltpu.roll(yface[t], cy - 1 - 2 * u, axis=1), 0.0))
                total = flux32[at, :] + jnp.concatenate(fix, axis=0)
                flux32[at, :] = total
                flux_out[at, :] = total.astype(BF16)
                return carry

            for i in range(4):
                outer(i, 0)

        def take(i16, acc, c=c):
            for u in range(16):
                i = i16 * 16 + u
                cell = cands[a, b, i]
                row = lax.div(cell, cy)
                found = flux32[pl.ds(c * per * zx + row, per, stride=zx), :]
                value = pltpu.roll(found, lax.rem(i + cy - (cell - row * cy), cy), axis=1)
                acc = jnp.where(lane_k == i, value, acc)
            return acc

        rowst[c * per : (c + 1) * per, :] = lax.fori_loop(0, k_count // 16, take, jnp.zeros((per, cy), F32))

    picked = rowst[...].T[:k_count]
    high = picked.astype(BF16).astype(F32)
    mine = jnp.concatenate([high, picked - high], axis=1).astype(BF16)
    g1[b] = mine

    def g1_copy(d, slot, device):
        return remote(g1.at[slot], g1.at[slot], g1send.at[d], g1recv.at[d], device)

    for d in range(1, ngy):
        g1_copy(d, b, (a, lax.rem(b + d, ngy))).start()
    for d in range(1, ngy):
        g1_copy(d, lax.rem(b + ngy - d, ngy), (a, lax.rem(b + d, ngy))).wait_recv()

    groups = ngy // 2
    for j in range(groups):
        kept = merge(onehot[a * groups + j], g1[2 * j], g1[2 * j + 1])
        g2[a, j] = kept.astype(BF16)
    core = lax.rem(b, 2)
    twin = (a, b + 1 - 2 * core)
    own = pl.ds(core * half, half)
    other = pl.ds((1 - core) * half, half)

    def g2_copy(d, slot, device):
        return remote(g2.at[slot, own], g2.at[slot, own], g2send.at[d], g2recv.at[d], device)

    def sib_copy(d, slot, part):
        return remote(g2.at[slot, part], g2.at[slot, part], sibsend.at[d], sibrecv.at[d], twin)

    for d in range(1, ngx):
        g2_copy(d, a, (lax.rem(a + d, ngx), b)).start()
    for d in range(1, ngx):
        slot = lax.rem(a + ngx - d, ngx)
        g2_copy(d, slot, (lax.rem(a + d, ngx), b)).wait_recv()
        sib_copy(d, slot, own).start()
    for d in range(1, ngx):
        sib_copy(d, lax.rem(a + ngx - d, ngx), other).wait_recv()

    for side in range(2):
        kx_copy(side).wait_send()
        y_copy(side).wait_send()
        ky_copy(side).wait_send()
        for c in range(CHUNKS):
            x_copy(side, c).wait_send()
    for d in range(1, ngy):
        g1_copy(d, b, (a, lax.rem(b + d, ngy))).wait_send()
    for d in range(1, ngx):
        g2_copy(d, a, (lax.rem(a + d, ngx), b)).wait_send()
        sib_copy(d, lax.rem(a + ngx - d, ngx), own).wait_send()


def solution(mesh):
    ngx, ngy = mesh.shape["gx"], mesh.shape["gy"]

    def local(states, class_map, perm_table, candidates, merge_order):
        _, k, planes, cx, cy = states.shape
        zx = planes * cx
        nodes = merge_order.shape[0]
        padded = (nodes + 7) // 8 * 8
        edge = 2 * (k // CHUNKS) * planes
        blocks = k * planes // (cy // 2)
        vmem = pl.BlockSpec(memory_space=pltpu.VMEM)
        hbm = pl.BlockSpec(memory_space=pltpu.HBM)
        dma = pltpu.SemaphoreType.DMA
        tiles = ngx * ngy
        flux, lowest, hots = pl.pallas_call(
            functools.partial(kernel, ngx, ngy, k, planes, cx, cy),
            out_shape=(
                jax.ShapeDtypeStruct((k * zx, cy), BF16),
                jax.ShapeDtypeStruct((ngx, ngy // 2, k, 2 * k), BF16),
                jax.ShapeDtypeStruct((nodes - tiles // 2, k, 2 * k), BF16),
            ),
            in_specs=[hbm] * 5,
            out_specs=(vmem,) * 3,
            scratch_shapes=[
                pltpu.VMEM((2, k * zx, cy), BF16),
                pltpu.VMEM((zx, cy), jnp.int32),
                pltpu.SMEM(perm_table.shape, F32),
                pltpu.SMEM(candidates.shape, jnp.int32),
                pltpu.VMEM((nodes, 2 * k), jnp.int32),
                pltpu.VMEM((k, cy), F32),
                dma((CHUNKS + 4,)),
                pltpu.VMEM((2, k * zx, cy), F32),
                pltpu.VMEM((k * zx, cy), F32),
                pltpu.VMEM((zx, cy), F32),
                pltpu.VMEM((planes, cx, cy), F32),
                pltpu.VMEM((planes, cx, cy), F32),
                pltpu.VMEM((planes - 1, cx, cy), F32),
                pltpu.VMEM((2, CHUNKS, edge, cy), BF16),
                pltpu.VMEM((2, CHUNKS, edge, cy), BF16),
                pltpu.VMEM((2, planes, cy), F32),
                pltpu.VMEM((2, planes, cy), F32),
                pltpu.VMEM((2 * blocks * cx, cy), BF16),
                pltpu.VMEM((2, 2 * blocks * cx, cy), BF16),
                pltpu.VMEM((cx, cy), F32),
                pltpu.VMEM((2, cx, cy), F32),
                pltpu.VMEM((blocks, cx, cy), F32),
                pltpu.VMEM((padded, 2 * k), F32),
                pltpu.VMEM((tiles // 2, k, 2 * k), BF16),
                pltpu.VMEM((ngy, k, 2 * k), BF16),
                dma((2, CHUNKS + 1)),
                dma((2, CHUNKS + 1)),
                dma((4,)),
                dma((4,)),
                dma((ngy,)),
                dma((ngy,)),
                dma((ngx,)),
                dma((ngx,)),
                dma((ngx,)),
                dma((ngx,)),
            ],
            compiler_params=pltpu.CompilerParams(
                collective_id=0, has_side_effects=True, vmem_limit_bytes=32 * 1024 * 1024
            ),
        )(*(
            pltpu.with_memory_space_constraint(x, pltpu.HBM)
            for x in (states.reshape(2, k * zx, cy), class_map.reshape(zx, cy), perm_table, candidates, merge_order)
        ))
        flux, kept = pl.pallas_call(
            functools.partial(finish, k),
            out_shape=(
                jax.ShapeDtypeStruct((k * zx, cy), BF16),
                jax.ShapeDtypeStruct((nodes, k, k), F32),
            ),
            in_specs=[vmem] * 3,
            out_specs=(hbm, hbm),
            scratch_shapes=[pltpu.VMEM((nodes, k, k), F32), dma((3,))],
            compiler_params=pltpu.CompilerParams(vmem_limit_bytes=24 * 1024 * 1024),
        )(flux, lowest, hots)
        return flux.reshape(k, planes, cx, cy), kept

    in_specs = (P(None, None, None, "gx", "gy"), P(None, "gx", "gy"), P(), P(), P())
    out_specs = (P(None, None, "gx", "gy"), P())
    return jax.shard_map(local, mesh=mesh, in_specs=in_specs, out_specs=out_specs, check_vma=False)
```
